128 devices in a mesh: user: 8 (over x, z_hi), item: 16 (over z_lo, y, core).
Axes of the slice: x: 4, y: 4, z: 4 (z_hi: 2, z_lo: 2; z = z_hi * 2 + z_lo), core: 2. Of those that a mesh axis runs over, the one named last changes fastest.
Arguments:
- counts: int32 [16384, 24576], P('user', 'item'), may hold values from 0 to 3
- user_factors: bfloat16 [16384, 256], P('user', 'item'), may hold values from -1.1953125 to 1.1953125
- item_factors: bfloat16 [24576, 256], P('item', 'user'), may hold values from -1.1953125 to 1.1953125
- alpha_scale: float32 [1], replicated, may hold values from 0.5 to 2
Outputs:
- user_new: float32 [16384, 256], P('user', 'item')
- item_new: float32 [24576, 256], P('item', 'user')
The draws below stay inside these ranges and needn't reach their ends.
All inputs are finite; a program needn't handle non-finite values.
Results may differ from the reference program's by a relative error of at most 0.0021.
Values may be sent and summed in bfloat16 or wider, within the bound.
A program may use at most 128 MiB of HBM per device.

```python
import math
import jax
import jax.numpy as jnp
from jax import lax

D = 256
UD = 2048
USERS = 16384
ITEMS = 24576


def touch_ends(result, rng, low, high):
    longest = result.shape.index(max(result.shape))
    spots = []
    for shift in (0, 1):
        where = [jax.random.randint(jax.random.fold_in(rng, axis), (), 0, length) for axis, length in enumerate(result.shape)]
        where[longest] = (where[longest] + shift) % result.shape[longest]
        spots.append(tuple(where))
    return result.at[spots[0]].set(low).at[spots[1]].set(high)


def steps_of(own_key, shape, shards, low, top_value):
    loudness = 1.0
    for axis_at, blocks in shards:
        heights = jax.random.uniform(jax.random.fold_in(jax.random.fold_in(own_key, 6), axis_at), (blocks,), jnp.float32, low / len(shards), top_value / len(shards))
        loudness = loudness * jnp.repeat(jnp.exp(heights), shape[axis_at] // blocks).reshape((-1,) + (1,) * (len(shape) - 1 - axis_at))
    return loudness


def scatter_about(own_key, dims, scale, limit, shards=(), held_as=jnp.bfloat16):
    level = steps_of(own_key, dims, shards, -0.22, 0.18) if shards else 1.0
    array = jax.random.normal(own_key, dims, jnp.float32) * scale * level
    return jnp.minimum(jnp.maximum(array, -limit), limit).astype(held_as)


def setup_inputs(seed: int = 0) -> dict:
    arg_keys = jax.random.split(jax.random.key(seed), 5)
    counts = touch_ends(jax.random.randint(arg_keys[0], (USERS, ITEMS), 0, 4), jax.random.fold_in(arg_keys[0], 1), 0, 3).astype(jnp.int32)
    user_factors = scatter_about(arg_keys[1], (USERS, D), 0.2, 1.1953125, ((0, 8), (1, 16)))
    item_factors = scatter_about(arg_keys[2], (ITEMS, D), 0.2, 1.1953125, ((0, 16), (1, 8)))
    alpha_scale = jnp.clip(jnp.exp(jax.random.uniform(arg_keys[3], (1,), jnp.float32, math.log(0.5), math.log(2.0))), 0.5, 2.0)
    return dict(counts=counts, user_factors=user_factors, item_factors=item_factors, alpha_scale=alpha_scale)


reg_weight = 1.0

def newton(gram_matrix, gradient):
    bound = 0.25 * gram_matrix + reg_weight * jnp.eye(gram_matrix.shape[0], dtype=jnp.float32)
    factor_low = jnp.linalg.cholesky(bound)
    return jax.scipy.linalg.cho_solve((factor_low, True), gradient.T).T

def coefficients(count_block, scale, left, right):
    scores = jnp.dot(left.astype(jnp.float32), right.T.astype(jnp.float32), preferred_element_type=jnp.float32)
    weight = scale * count_block.astype(jnp.float32)
    return (weight - (1.0 + weight) * jax.nn.sigmoid(scores)).astype(jnp.bfloat16)

def reference(counts, user_factors, item_factors, alpha_scale):
    scale = alpha_scale[0]
    blocks = USERS // UD
    count_blocks = counts.reshape(blocks, UD, ITEMS)
    user_blocks = user_factors.reshape(blocks, UD, D)

    def user_block(couple):
        count_block, factor_block = couple
        coefficient = coefficients(count_block, scale, factor_block, item_factors)
        return jnp.dot(coefficient.astype(jnp.float32), item_factors.astype(jnp.float32), preferred_element_type=jnp.float32)
    gradient = lax.map(user_block, (count_blocks, user_blocks)).reshape(USERS, D)
    gradient = gradient - reg_weight * user_factors.astype(jnp.float32)
    gram_items = jnp.dot(item_factors.T.astype(jnp.float32), item_factors.astype(jnp.float32), preferred_element_type=jnp.float32)
    user_new = user_factors.astype(jnp.float32) + newton(gram_items, gradient)
    user_half = user_new.astype(jnp.bfloat16)
    half_blocks = user_half.reshape(blocks, UD, D)

    def item_block(running, couple):
        count_block, factor_block = couple
        coefficient = coefficients(count_block, scale, factor_block, item_factors)
        return (running + jnp.dot(coefficient.T.astype(jnp.float32), factor_block.astype(jnp.float32), preferred_element_type=jnp.float32), None)
    item_grad, unused = lax.scan(item_block, jnp.zeros((ITEMS, D), jnp.float32), (count_blocks, half_blocks))
    item_grad = item_grad - reg_weight * item_factors.astype(jnp.float32)
    gram_users = jnp.dot(user_half.T.astype(jnp.float32), user_half.astype(jnp.float32), preferred_element_type=jnp.float32)
    item_new = item_factors.astype(jnp.float32) + newton(gram_users, item_grad)
    return (user_new, item_new)
```

```python
import functools

import jax
import jax.numpy as jnp
from jax import lax
from jax.experimental import pallas as pl
from jax.experimental.pallas import tpu as pltpu
from jax.sharding import PartitionSpec as P

MESH = pl.DeviceIdType.MESH
EXACT = lax.Precision.HIGHEST
F32 = jnp.float32
BF16 = jnp.bfloat16
TN = (((0,), (0,)), ((), ()))
REG = 1.0
PANEL = 32
LANES = 128
TILE = 16


def eye(n):
    return lax.broadcasted_iota(jnp.int32, (n, n), 0) == lax.broadcasted_iota(
        jnp.int32, (n, n), 1
    )


def invert(a_ref):
    n = a_ref.shape[0]
    ri = lax.broadcasted_iota(jnp.int32, (n, n), 0)
    ci = lax.broadcasted_iota(jnp.int32, (n, n), 1)
    h = a_ref[...]
    diagonal = jnp.where(ri == ci, h, 0.0)
    s_row = lax.rsqrt(jnp.sum(diagonal, axis=0, keepdims=True))
    s_col = lax.rsqrt(jnp.sum(diagonal, axis=1, keepdims=True))
    a_ref[...] = h * s_row * s_col
    lr = lax.broadcasted_iota(jnp.int32, (PANEL, n), 0)
    lc = lax.broadcasted_iota(jnp.int32, (PANEL, n), 1)
    sub = lax.broadcasted_iota(jnp.int32, (PANEL, LANES), 0)
    lane = lax.broadcasted_iota(jnp.int32, (PANEL, LANES), 1)

    def block(k, carry):
        first = pl.multiple_of(k * PANEL, PANEL)
        panel = a_ref[pl.ds(first, PANEL), :]
        d = pltpu.roll(panel, lax.rem(n - k * PANEL, n), 1)[:, :LANES]
        for g in range(PANEL // 8):
            cols = [
                jnp.broadcast_to(d[:, 8 * g + m : 8 * g + m + 1], (PANEL, LANES))
                for m in range(8)
            ]
            for m in range(8):
                j = 8 * g + m
                c = cols[m]
                p = 1.0 / c[j : j + 1, :]
                for mm in range(m + 1, 8):
                    y = cols[mm][j : j + 1, :] * p
                    cols[mm] = jnp.where(sub == j, y, cols[mm] - c * y)
                y = jnp.where(lane[:1] == j, 1.0, d[j : j + 1, :]) * p
                d = jnp.where(sub == j, y, jnp.where(lane == j, 0.0, d) - c * y)
        y = panel - jnp.where(lc == lr + k * PANEL, 1.0, 0.0)
        t = jnp.dot(d[:, :PANEL], y, precision=EXACT, preferred_element_type=F32)
        inside = (ri == ci) & (ri >= k * PANEL) & (ri < k * PANEL + PANEL)
        a_ref[...] = (
            a_ref[...]
            - lax.dot_general(y, t, TN, precision=EXACT, preferred_element_type=F32)
            - jnp.where(inside, 2.0, 0.0)
        )
        return carry

    lax.fori_loop(0, n // PANEL, block, 0)
    a_ref[...] = -a_ref[...] * s_row * s_col


def level(x):
    top = jnp.maximum(jnp.max(jnp.abs(x), axis=0, keepdims=True), 1e-30)
    return jnp.ceil(jnp.log2(top) - 14.99)


def pack(x, into, n):
    power = level(x)
    whole = jnp.clip(jnp.round(x * jnp.exp2(-power)), -32767.0, 32767.0)
    into[:n, :] = whole.astype(jnp.int32).astype(jnp.int16)
    into[n:, :] = jnp.broadcast_to(power, (TILE, x.shape[1])).astype(jnp.int32).astype(jnp.int16)


def unpack(ref, n):
    power = ref[n:, :].astype(jnp.int32).astype(F32)[:1]
    return ref[:n, :].astype(jnp.int32).astype(F32) * jnp.exp2(power)


def kernel(
    nu, ni,
    alpha_ref, u_in, i_in, counts_hbm, u_out, i_out,
    counts, ut, it, un, inat, cf,
    keep, sib_send, sib_recv, rs1_send, rs1_recv, gi_part, gi_recv, gi,
    uh, uht, u_new,
    gu_part, gu_recv, gu,
    rs2_send, rs2_recv, i_new,
    counts_sem, item_send, item_recv, line_send, line_recv, sib_sem, sib_done, user_send, user_recv,
):
    mu, mi = lax.axis_index("user"), lax.axis_index("item")
    d, users = ut.shape
    items = it.shape[1]
    nk = ni // 2
    place, core = mi // 2, lax.rem(mi, 2)
    sibling = mi + 1 - 2 * core
    wu, wi = d // ni, d // nu
    own_u, own_i = users // ni, items // nu
    pair_u, pair_i = 2 * own_u, 2 * own_i
    i_pairs = nu // 2

    def rows(n, k):
        return pl.ds(pl.multiple_of(k * n, n), n)

    def item_peer(off):
        return lax.rem(mi + off, ni)

    def user_peer(off):
        return lax.rem(mu + off, nu)

    def after(off):
        return lax.rem(place + off, nk)

    def before(off):
        return lax.rem(place + nk - off, nk)

    def copy(src, dst, sent, landed, device):
        return pltpu.make_async_remote_copy(
            src_ref=src, dst_ref=dst, send_sem=sent, recv_sem=landed,
            device_id=device, device_id_type=MESH,
        )

    def over_item(kind, off, src, dst):
        return copy(src, dst, item_send.at[kind, off], item_recv.at[kind, off], (mu, item_peer(off)))

    def over_line(kind, off, src, dst):
        return copy(src, dst, line_send.at[kind, off], line_recv.at[kind, off], (mu, 2 * after(off) + core))

    def over_chip(kind, k, src, dst):
        return copy(src, dst, sib_sem.at[kind, k], sib_done.at[kind, k], (mu, sibling))

    def over_user(kind, off, src, dst):
        return copy(src, dst, user_send.at[kind, off], user_recv.at[kind, off], (user_peer(off), mi))

    def ag_user(off, k):
        return over_line(0, off, u_in, ut.at[rows(wu, 2 * k + core), :])

    def ag_user_own():
        return over_chip(0, place, u_in, ut.at[rows(wu, mi), :])

    def ag_user_on(k, c):
        part = ut.at[rows(wu, 2 * k + c), :]
        return over_chip(0, k, part, part)

    def rs1(off):
        return over_line(1, off, rs1_send.at[after(off)], rs1_recv.at[off])

    def halves(k):
        return over_chip(1, k, sib_send.at[k], sib_recv.at[k])

    def gi_rs(off):
        return over_item(0, off, gi_part.at[rows(wu, item_peer(off)), :], gi_recv.at[off])

    def gi_ag(off, who):
        return over_item(1, off, gi.at[rows(wu, who), :], gi.at[rows(wu, who), :])

    def ag_half(off, k):
        part = uh.at[rows(own_u, 2 * k + core), :]
        return over_line(2, off, part, part)

    def ag_half_on(k, c):
        part = uh.at[rows(own_u, 2 * k + c), :]
        return over_chip(2, k, part, part)

    def out_user(off, who):
        return over_item(
            2, off, u_new.at[rows(wu, item_peer(off)), :], u_out.at[:, rows(own_u, who)]
        )

    def ag_item(off, who):
        return over_user(0, off, i_in, it.at[rows(wi, who), :])

    def rs2(off):
        return over_user(1, off, rs2_send.at[user_peer(off)], rs2_recv.at[off])

    def gu_rs(off):
        return over_user(2, off, gu_part.at[rows(wi, user_peer(off)), :], gu_recv.at[off])

    def gu_ag(off, who):
        return over_user(3, off, gu.at[rows(wi, who), :], gu.at[rows(wi, who), :])

    def out_item(off, who):
        return over_user(4, off, i_new.at[rows(wi, user_peer(off)), :], i_out.at[who])

    def each(n, what, first=1):
        def step(off, carry):
            what(off)
            return carry

        lax.fori_loop(first, n, step, 0)

    def from_item(off):
        return lax.rem(mi + ni - off, ni)

    def from_user(off):
        return lax.rem(mu + nu - off, nu)

    def counts_copy(k):
        part = rows(pair_u, k)
        return pltpu.make_async_copy(
            counts_hbm.at[part, :], counts.at[part, :], counts_sem.at[k]
        )

    for k in range(nk):
        counts_copy(k).start()

    barrier = pltpu.get_barrier_semaphore()
    each(ni, lambda off: pl.semaphore_signal(barrier, inc=1, device_id=(mu, item_peer(off)), device_id_type=MESH))
    each(nu, lambda off: pl.semaphore_signal(barrier, inc=1, device_id=(user_peer(off), mi), device_id_type=MESH))
    pl.semaphore_wait(barrier, ni + nu - 2)

    each(nu, lambda off: ag_item(off, mu).start())
    ag_user_own().start()
    each(nk, lambda off: ag_user(off, place).start())
    it[rows(wi, mu), :] = i_in[...]
    ut[rows(wu, mi), :] = u_in[...]

    each(nu, lambda off: ag_item(off, from_user(off)).wait_recv())
    inat[...] = it[...].T
    gi_part[...] = jnp.dot(it[...], inat[...], preferred_element_type=F32)
    each(ni, lambda off: gi_rs(off).start())

    def user_arrived(off):
        ag_user(off, before(off)).wait_recv()
        ag_user_on(before(off), core).start()

    each(nk, user_arrived)
    each(nk, lambda k: ag_user_on(k, 1 - core).wait_recv(), 0)
    un[...] = ut[...].T * jnp.asarray(0.5, BF16)
    for k in range(nk):
        counts_copy(k).wait()

    half_scale = alpha_ref[0] * 0.5

    def coefficients(half_left, part, into):
        step = 256
        for t in range(items // step):
            cols = slice(t * step, (t + 1) * step)
            s = jnp.dot(half_left, it[:, cols], preferred_element_type=F32)
            a = counts[part, cols].astype(F32) * half_scale
            cf[into, cols] = ((a - 0.5) - (a + 0.5) * jnp.tanh(s)).astype(BF16)

    def user_pair(k):
        part = rows(pair_u, k)
        coefficients(un[part, :], part, part)
        grad = jnp.dot(cf[part, :], inat[...], preferred_element_type=F32)
        lower, upper = grad[:own_u], grad[own_u:]
        keep[k] = jnp.where(core == 0, lower, upper)
        sib_send[k] = jnp.where(core == 0, upper, lower)
        halves(k).start()

    def on_to_owner(off):
        k = after(off)
        halves(k).wait_recv()
        pack(keep[k] + sib_recv[k], rs1_send.at[k], own_u)
        rs1(off).start()

    def first_pass(off, carry):
        user_pair(after(off))
        on_to_owner(off - 1)
        return carry

    user_pair(after(1))
    lax.fori_loop(2, 4, first_pass, 0)

    mine = rows(wu, mi)
    each(ni, lambda off: gi_rs(off).wait_recv())
    total = gi_part[mine, :]
    for off in range(1, ni):
        total += gi_recv[off]
    gi[mine, :] = total
    each(ni, lambda off: gi_ag(off, mi).start())

    lax.fori_loop(4, nk, first_pass, 0)
    user_pair(place)
    on_to_owner(nk - 1)

    each(ni, lambda off: gi_ag(off, from_item(off)).wait_recv())
    each(ni, lambda off: gi_rs(off).wait_send())
    gi_part[...] = 0.25 * gi[...] + jnp.where(eye(d), REG, 0.0)
    invert(gi_part)

    halves(place).wait_recv()
    grad = keep[place] + sib_recv[place]
    each(nk, lambda off: rs1(off).wait_recv())
    for off in range(1, nk):
        grad += unpack(rs1_recv.at[off], own_u)
    own = un[rows(own_u, mi), :].astype(F32) * 2.0
    grad = grad - REG * own
    new = own + jnp.dot(grad, gi_part[...], precision=EXACT, preferred_element_type=F32)
    uh[rows(own_u, mi), :] = new.astype(BF16)
    ag_half_on(place, core).start()
    each(nk, lambda off: ag_half(off, place).start())
    u_new[...] = new.T
    u_out[:, rows(own_u, mi)] = u_new[mine, :]
    each(ni, lambda off: out_user(off, mi).start())

    def half_arrived(off):
        ag_half(off, before(off)).wait_recv()
        ag_half_on(before(off), core).start()

    def second_pass(k):
        ag_half_on(k, 1 - core).wait_recv()
        part = rows(pair_u, k)
        half = uh[part, :]
        uht[:, part] = half.T
        coefficients(half * jnp.asarray(0.5, BF16), part, part)

    def second_step(off, carry):
        half_arrived(off + 1)
        second_pass(before(off))
        return carry

    lax.fori_loop(0, nk - 1, second_step, 0)
    second_pass(before(nk - 1))

    gu_part[...] = jnp.dot(uht[...], uh[...], preferred_element_type=F32)
    each(nu, lambda off: gu_rs(off).start())

    def item_pair(q, carry):
        g = jnp.dot(uht[...], cf[:, rows(pair_i, q)], preferred_element_type=F32)
        g = g.T
        pack(g[:own_i], rs2_send.at[2 * q], own_i)
        pack(g[own_i:], rs2_send.at[2 * q + 1], own_i)
        return carry

    lax.fori_loop(0, i_pairs, item_pair, 0)

    slab = rows(wi, mu)
    each(nu, lambda off: gu_rs(off).wait_recv())
    total = gu_part[slab, :]
    for off in range(1, nu):
        total += gu_recv[off]
    gu[slab, :] = total
    each(nu, lambda off: gu_ag(off, mu).start())
    each(nu, lambda off: rs2(off).start())
    each(nu, lambda off: gu_ag(off, from_user(off)).wait_recv())
    each(nu, lambda off: gu_rs(off).wait_send())
    gu_part[...] = 0.25 * gu[...] + jnp.where(eye(d), REG, 0.0)
    invert(gu_part)

    grad = unpack(rs2_send.at[mu], own_i)
    each(nu, lambda off: rs2(off).wait_recv())
    for off in range(1, nu):
        grad += unpack(rs2_recv.at[off], own_i)
    own = inat[rows(own_i, mu), :].astype(F32)
    grad = grad - REG * own
    new = own + jnp.dot(grad, gu_part[...], precision=EXACT, preferred_element_type=F32)
    i_new[...] = new.T
    each(nu, lambda off: out_item(off, mu).start())
    i_out[mu] = i_new[slab, :]

    each(ni, lambda off: out_user(off, from_item(off)).wait_recv())
    each(nu, lambda off: out_item(off, from_user(off)).wait_recv())

    def drain_item(off):
        gi_ag(off, mi).wait_send()
        out_user(off, mi).wait_send()

    def drain_line(off):
        ag_user(off, place).wait_send()
        rs1(off).wait_send()
        ag_half(off, place).wait_send()

    def drain_chip(k):
        ag_user_on(k, core).wait_send()
        halves(k).wait_send()
        ag_half_on(k, core).wait_send()

    def drain_user(off):
        ag_item(off, mu).wait_send()
        rs2(off).wait_send()
        gu_ag(off, mu).wait_send()
        out_item(off, mu).wait_send()

    each(ni, drain_item)
    each(nk, drain_line)
    each(nk, drain_chip, 0)
    each(nu, drain_user)


def on_device(nu, ni, counts, user_factors, item_factors, alpha_scale):
    users, items = counts.shape
    d = user_factors.shape[1] * ni
    nk = ni // 2
    wu, wi, own_u, own_i = d // ni, d // nu, users // ni, items // nu
    vmem = pl.BlockSpec(memory_space=pltpu.VMEM)
    spare, dma = pltpu.VMEM, pltpu.SemaphoreType.DMA
    u_out, i_out = pl.pallas_call(
        functools.partial(kernel, nu, ni),
        out_shape=(
            jax.ShapeDtypeStruct((wu, users), F32),
            jax.ShapeDtypeStruct((nu, wi, own_i), F32),
        ),
        in_specs=[
            pl.BlockSpec(memory_space=pltpu.SMEM), vmem, vmem, pl.BlockSpec(memory_space=pl.ANY),
        ],
        out_specs=(vmem, vmem),
        scratch_shapes=[
            spare((users, items), jnp.int32),
            spare((d, users), BF16), spare((d, items), BF16),
            spare((users, d), BF16), spare((items, d), BF16),
            spare((users, items), BF16),
            spare((nk, own_u, d), F32), spare((nk, own_u, d), F32), spare((nk, own_u, d), F32),
            spare((nk, own_u + TILE, d), jnp.int16), spare((nk, own_u + TILE, d), jnp.int16),
            spare((d, d), F32), spare((ni, wu, d), F32), spare((d, d), F32),
            spare((users, d), BF16), spare((d, users), BF16), spare((d, own_u), F32),
            spare((d, d), F32), spare((nu, wi, d), F32), spare((d, d), F32),
            spare((nu, own_i + TILE, d), jnp.int16), spare((nu, own_i + TILE, d), jnp.int16),
            spare((d, own_i), F32),
            dma((nk,)), dma((3, ni)), dma((3, ni)), dma((3, nk)), dma((3, nk)),
            dma((3, nk)), dma((3, nk)), dma((5, nu)), dma((5, nu)),
        ],
        compiler_params=pltpu.CompilerParams(
            collective_id=0, has_side_effects=True, vmem_limit_bytes=60 << 20
        ),
    )(alpha_scale, user_factors.T, item_factors.T, counts)
    return u_out.T, i_out.transpose(0, 2, 1).reshape(items, wi)


def solution(mesh):
    in_specs = (P("user", "item"), P("user", "item"), P("item", "user"), P())
    out_specs = (P("user", "item"), P("item", "user"))
    return jax.shard_map(
        functools.partial(on_device, mesh.shape["user"], mesh.shape["item"]),
        mesh=mesh, in_specs=in_specs, out_specs=out_specs, check_vma=False,
    )
```

```python
import functools

import jax
import jax.numpy as jnp
from jax import lax
from jax.experimental import pallas as pl
from jax.experimental.pallas import tpu as pltpu
from jax.sharding import PartitionSpec as P

MESH = pl.DeviceIdType.MESH
EXACT = lax.Precision.HIGHEST
F32 = jnp.float32
BF16 = jnp.bfloat16
TN = (((0,), (0,)), ((), ()))
NT = (((1,), (1,)), ((), ()))
REG = 1.0
PANEL = 32
LANES = 128
TILE = 16
STEPS_BESIDE = 6
HOPS = (
    (1, 0, 0, 0, None, None),
    (-1, 0, 0, 0, None, None),
    (0, 1, 0, 0, None, None),
    (1, 0, -1, 0, 0, 0),
    (-1, 0, 1, 0, 1, 1),
    (1, 1, -1, 0, 0, 0),
    (-1, 1, 1, 0, 1, 1),
    (1, 0, 0, 1, None, 2),
    (-1, 0, 0, 1, None, 2),
)


def eye(n):
    return lax.broadcasted_iota(jnp.int32, (n, n), 0) == lax.broadcasted_iota(
        jnp.int32, (n, n), 1
    )


def scales(h):
    diagonal = jnp.where(eye(h.shape[0]), h, 0.0)
    return (
        lax.rsqrt(jnp.sum(diagonal, axis=0, keepdims=True)),
        lax.rsqrt(jnp.sum(diagonal, axis=1, keepdims=True)),
    )


def eliminations(d):
    sub = lax.broadcasted_iota(jnp.int32, (PANEL, LANES), 0)
    lane = lax.broadcasted_iota(jnp.int32, (PANEL, LANES), 1)

    def step(j):
        m = j % 8
        now = d["now"]
        if m == 0:
            d["cols"] = [jnp.broadcast_to(now[:, j + q : j + q + 1], (PANEL, LANES)) for q in range(8)]
        cols = d["cols"]
        c = cols[m]
        p = 1.0 / c[j : j + 1, :]
        for mm in range(m + 1, 8):
            y = cols[mm][j : j + 1, :] * p
            cols[mm] = jnp.where(sub == j, y, cols[mm] - c * y)
        y = jnp.where(lane[:1] == j, 1.0, now[j : j + 1, :]) * p
        d["now"] = jnp.where(sub == j, y, jnp.where(lane == j, 0.0, now) - c * y)

    return [functools.partial(step, j) for j in range(PANEL)]


class Sweep:
    def __init__(self, a_ref, u_ref, y_ref):
        self.a, self.u, self.y = a_ref, u_ref, y_ref
        self.n = a_ref.shape[0]

    def begin(self, h):
        s_row, s_col = scales(h)
        self.a[...] = h * s_row * s_col
        self.u[...] = jnp.zeros_like(self.u)
        self.y[...] = jnp.zeros_like(self.y)

    def update(self, k):
        ri = lax.broadcasted_iota(jnp.int32, (self.n, self.n), 0)
        inside = eye(self.n) & (ri >= (k - 1) * PANEL) & (ri < k * PANEL)
        return jnp.dot(self.u[:, :PANEL], self.y[...], precision=EXACT, preferred_element_type=F32) + jnp.where(inside, 2.0, 0.0)

    def block(self, k, beside=()):
        n = self.n
        rows = pl.ds(pl.multiple_of(k * PANEL, PANEL), PANEL)
        panel = self.a[rows, :] - jnp.dot(self.u[rows, :PANEL], self.y[...], precision=EXACT, preferred_element_type=F32)
        d = {"now": pltpu.roll(panel, lax.rem(n - k * PANEL, n), 1)[:, :LANES]}
        steps = eliminations(d)
        for work in beside[:-1]:
            work()
            for _ in range(STEPS_BESIDE):
                if steps:
                    steps.pop(0)()
        for step in steps:
            step()
        for work in beside[-1:]:
            work()
        self.a[...] = self.a[...] - self.update(k)
        lr = lax.broadcasted_iota(jnp.int32, (PANEL, n), 0)
        lc = lax.broadcasted_iota(jnp.int32, (PANEL, n), 1)
        y = panel - jnp.where(lc == lr + k * PANEL, 1.0, 0.0)
        self.y[...] = y
        self.u[:, :PANEL] = lax.dot_general(y, d["now"][:, :PANEL], TN, precision=EXACT, preferred_element_type=F32)

    def end(self, h):
        s_row, s_col = scales(h)
        self.a[...] = (self.update(self.n // PANEL) - self.a[...]) * s_row * s_col


def level(x):
    top = jnp.maximum(jnp.max(jnp.abs(x), axis=0, keepdims=True), 1e-30)
    return jnp.ceil(jnp.log2(top) - 14.99)


def pack(x, into, n):
    power = level(x)
    whole = jnp.clip(jnp.round(x * jnp.exp2(-power)), -32767.0, 32767.0)
    into[:n, :] = whole.astype(jnp.int32).astype(jnp.int16)
    into[n:, :] = jnp.broadcast_to(power, (TILE, x.shape[1])).astype(jnp.int32).astype(jnp.int16)


def unpack(ref, n):
    power = ref[n:, :].astype(jnp.int32).astype(F32)[:1]
    return ref[:n, :].astype(jnp.int32).astype(F32) * jnp.exp2(power)


def kernel(
    nu, ni,
    alpha_ref, u_in, i_in, counts_hbm, u_out, i_out,
    counts, ut, it, inat, cf,
    keep, sib_send, sib_recv, rs1_send, rs1_recv, gi_part, gi_recv, gi,
    uh, uht, u_new,
    gu_rows, gu,
    rs2_send, rs2_recv, i_new,
    inv_a, inv_u, inv_y,
    counts_sem, item_send, item_recv, line_send, line_recv, sib_sem, sib_done, user_send, user_recv,
    ring_send, ring_recv,
):
    mu, mi = lax.axis_index("user"), lax.axis_index("item")
    d, users = ut.shape
    items = it.shape[1]
    nk = ni // 2
    place, core = mi // 2, lax.rem(mi, 2)
    sibling = mi + 1 - 2 * core
    wu, wi = d // ni, d // nu
    own_u, own_i = users // ni, items // nu
    pair_u, pair_i = 2 * own_u, 2 * own_i
    i_pairs = nu // 2

    def rows(n, k):
        return pl.ds(pl.multiple_of(k * n, n), n)

    def item_peer(off):
        return lax.rem(mi + off, ni)

    def user_peer(off):
        return lax.rem(mu + off, nu)

    def after(off):
        return lax.rem(place + off, nk)

    def chip_at(along, across):
        y, z = lax.rem(place, 4), place // 4
        return 4 * lax.rem(z + across + 2, 2) + lax.rem(y + along + 4, 4)

    def group_at(along, across):
        x, z = mu // 2, lax.rem(mu, 2)
        return 2 * lax.rem(x + along + 4, 4) + lax.rem(z + across + 2, 2)

    def copy(src, dst, sent, landed, device):
        return pltpu.make_async_remote_copy(
            src_ref=src, dst_ref=dst, send_sem=sent, recv_sem=landed,
            device_id=device, device_id_type=MESH,
        )

    def over_item(kind, off, src, dst):
        return copy(src, dst, item_send.at[kind, off], item_recv.at[kind, off], (mu, item_peer(off)))

    def over_line(kind, off, src, dst):
        return copy(src, dst, line_send.at[kind, off], line_recv.at[kind, off], (mu, 2 * after(off) + core))

    def over_chip(kind, k, src, dst):
        return copy(src, dst, sib_sem.at[kind, k], sib_done.at[kind, k], (mu, sibling))

    def over_user(kind, off, src, dst):
        return copy(src, dst, user_send.at[kind, off], user_recv.at[kind, off], (user_peer(off), mi))

    class Gather:
        def __init__(self, kind, at, to, part):
            self.kind, self.at, self.to, self.part = kind, at, to, part

        def hop(self, slot):
            along, across, b_along, b_across, half, _ = HOPS[slot]
            ref = self.part(self.at(b_along, b_across), half)
            return copy(ref, ref, ring_send.at[self.kind, slot], ring_recv.at[self.kind, slot], self.to(self.at(along, across)))

        def landed(self, slot):
            along, across, b_along, b_across, half, _ = HOPS[slot]
            return self.part(self.at(b_along - along, b_across - across), half)

        def start(self):
            for slot in range(3):
                self.hop(slot).start()

        def arrived(self, slot):
            ref = self.landed(slot)
            copy(ref, ref, ring_send.at[self.kind, slot], ring_recv.at[self.kind, slot], self.to(self.at(0, 1))).wait_recv()
            for later in range(len(HOPS)):
                if HOPS[later][-1] == slot:
                    self.hop(later).start()

        def drain(self):
            for slot in range(len(HOPS)):
                self.hop(slot).wait_send()

    def item_part(k, half):
        if half is None:
            return it.at[rows(wi, k), :]
        return it.at[rows(wi // 2, 2 * k + half), :]

    def user_part_of(c):
        def part(k, half):
            if half is None:
                return ut.at[rows(wu, 2 * k + c), :]
            return ut.at[rows(wu, 2 * k + c), pl.ds(half * (users // 2), users // 2)]

        return part

    def half_part_of(c):
        def part(k, half):
            if half is None:
                return uh.at[rows(own_u, 2 * k + c), :]
            return uh.at[rows(own_u // 2, 4 * k + 2 * c + half), :]

        return part

    def same_core(k):
        return (mu, 2 * k + core)

    gather_items = Gather(0, group_at, lambda k: (k, mi), item_part)
    gather_users = Gather(1, chip_at, same_core, user_part_of(core))
    gather_half = Gather(2, chip_at, same_core, half_part_of(core))

    def passed_on(kind, slot, part_of, c):
        if slot == len(HOPS):
            ref = part_of(c)(place, None)
        else:
            along, across, b_along, b_across, half, _ = HOPS[slot]
            ref = part_of(c)(chip_at(b_along - along, b_across - across), half)
        return over_chip(kind, slot, ref, ref)

    def user_on(slot, c):
        return passed_on(0, slot, user_part_of, c)

    def half_on(slot, c):
        return passed_on(1, slot, half_part_of, c)

    own_slot = len(HOPS)

    def halves(k):
        return over_chip(2, k, sib_send.at[k], sib_recv.at[k])

    def rs1(off):
        return over_line(0, off, rs1_send.at[after(off)], rs1_recv.at[off])

    def gi_rs(off):
        return over_item(0, off, gi_part.at[rows(wu, item_peer(off)), :], gi_recv.at[off])

    def gi_ag(off, who):
        return over_item(1, off, gi.at[rows(wu, who), :], gi.at[rows(wu, who), :])

    def out_user(off, who):
        return over_item(
            2, off, u_new.at[rows(wu, item_peer(off)), :], u_out.at[:, rows(own_u, who)]
        )

    def gu_ag(off, who):
        return over_item(3, off, gu.at[rows(wu, who), :], gu.at[rows(wu, who), :])

    def rs2(off):
        return over_user(0, off, rs2_send.at[user_peer(off)], rs2_recv.at[off])

    def gu_rs(off, who):
        return over_user(1, off, gu_rows.at[who], gu_rows.at[who])

    def out_item(off, who):
        return over_user(2, off, i_new.at[rows(wi, user_peer(off)), :], i_out.at[who])

    def each(n, what, first=1):
        def step(off, carry):
            what(off)
            return carry

        lax.fori_loop(first, n, step, 0)

    def from_item(off):
        return lax.rem(mi + ni - off, ni)

    def from_user(off):
        return lax.rem(mu + nu - off, nu)

    def counts_copy(k):
        part = rows(pair_u, k)
        return pltpu.make_async_copy(
            counts_hbm.at[part, :], counts.at[part, :], counts_sem.at[k]
        )

    for k in range(nk):
        counts_copy(k).start()
    it[rows(wi, mu), :] = i_in[...]
    ut[rows(wu, mi), :] = u_in[...]

    barrier = pltpu.get_barrier_semaphore()
    each(ni, lambda off: pl.semaphore_signal(barrier, inc=1, device_id=(mu, item_peer(off)), device_id_type=MESH))
    each(nu, lambda off: pl.semaphore_signal(barrier, inc=1, device_id=(user_peer(off), mi), device_id_type=MESH))
    pl.semaphore_wait(barrier, ni + nu - 2)

    gather_items.start()
    gather_users.start()
    user_on(own_slot, core).start()
    for slot in range(2):
        gather_items.arrived(slot)
    for slot in range(2):
        gather_users.arrived(slot)
        user_on(slot, core).start()
    gather_items.arrived(2)
    gather_users.arrived(2)
    user_on(2, core).start()
    for slot in range(3, len(HOPS)):
        gather_items.arrived(slot)

    gi_part[...] = lax.dot_general(it[...], it[...], NT, preferred_element_type=F32)
    each(ni, lambda off: gi_rs(off).start())
    inat[...] = it[...].T

    for slot in range(3, len(HOPS)):
        gather_users.arrived(slot)
        user_on(slot, core).start()
    mine = rows(wu, mi)
    each(ni, lambda off: gi_rs(off).wait_recv())
    total = gi_part[mine, :]
    for off in range(1, ni):
        total += gi_recv[off]
    gi[mine, :] = total
    each(ni, lambda off: gi_ag(off, mi).start())

    for slot in range(len(HOPS) + 1):
        user_on(slot, 1 - core).wait_recv()
    for k in range(nk):
        counts_copy(k).wait()

    half_scale = alpha_ref[0] * 0.5

    def coefficients(half_left, part):
        step = 256

        def tile(t):
            cols = slice(t * step, (t + 1) * step)
            s = jnp.dot(half_left, it[:, cols], preferred_element_type=F32)
            a = counts[part, cols].astype(F32) * half_scale
            cf[part, cols] = ((a - 0.5) - (a + 0.5) * jnp.tanh(s)).astype(BF16)

        return [functools.partial(tile, t) for t in range(items // step)]

    def user_pair(k):
        part = rows(pair_u, k)

        def gradient():
            grad = jnp.dot(cf[part, :], inat[...], preferred_element_type=F32)
            lower, upper = grad[:own_u], grad[own_u:]
            keep[k] = jnp.where(core == 0, lower, upper)
            sib_send[k] = jnp.where(core == 0, upper, lower)

        return coefficients(ut[:, part].T * jnp.asarray(0.5, BF16), part) + [gradient]

    def on_to_owner(off):
        k = after(off)
        halves(k).wait_recv()
        pack(keep[k] + sib_recv[k], rs1_send.at[k], own_u)
        rs1(off).start()

    sweep = Sweep(inv_a, inv_u, inv_y)
    for work in user_pair(after(1)):
        work()
    halves(after(1)).start()
    each(ni, lambda off: gi_ag(off, from_item(off)).wait_recv())

    def hessian(gram):
        return 0.25 * gram[...] + jnp.where(eye(d), REG, 0.0)

    sweep.begin(hessian(gi))

    def first_pass(off, carry):
        sweep.block(off - 2, user_pair(after(off)))
        halves(after(off)).start()
        on_to_owner(off - 1)
        return carry

    lax.fori_loop(2, nk + 1, first_pass, 0)
    sweep.block(nk - 1)
    sweep.end(hessian(gi))

    halves(place).wait_recv()
    grad = keep[place] + sib_recv[place]
    each(nk, lambda off: rs1(off).wait_recv())
    for off in range(1, nk):
        grad += unpack(rs1_recv.at[off], own_u)
    own = ut[:, rows(own_u, mi)].T.astype(F32)
    grad = grad - REG * own
    new = own + jnp.dot(grad, inv_a[...], precision=EXACT, preferred_element_type=F32)
    uh[rows(own_u, mi), :] = new.astype(BF16)
    gather_half.start()
    half_on(own_slot, core).start()
    u_new[...] = new.T
    u_out[:, rows(own_u, mi)] = u_new[mine, :]

    def turn(k):
        part = rows(pair_u, k)
        uht[:, part] = uh[part, :].T

    def second_pass(k):
        part = rows(pair_u, k)
        half = uh[part, :]
        for work in coefficients(half * jnp.asarray(0.5, BF16), part):
            work()

    half_on(own_slot, 1 - core).wait_recv()
    second_pass(place)
    turn(place)
    for slot in range(3):
        gather_half.arrived(slot)
        half_on(slot, core).start()
    for slot in range(3):
        half_on(slot, 1 - core).wait_recv()

    def near(t, carry):
        k = chip_at(jnp.where(t == 0, -1, jnp.where(t == 1, 1, 0)), jnp.where(t == 2, 1, 0))
        second_pass(k)
        turn(k)
        return carry

    lax.fori_loop(0, 3, near, 0)
    for slot in range(3, len(HOPS)):
        gather_half.arrived(slot)
        half_on(slot, core).start()
    for slot in range(3, len(HOPS)):
        half_on(slot, 1 - core).wait_recv()

    def far(t):
        return chip_at(jnp.where(t < 2, 2, jnp.where(t == 2, 1, -1)), jnp.where(t == 0, 0, 1))

    def far_turn(t, carry):
        turn(far(t))
        return carry

    def far_pass(t, carry):
        second_pass(far(t))
        return carry

    lax.fori_loop(0, 4, far_turn, 0)
    gu_rows[mu] = jnp.dot(uht[mine, :], uh[...], preferred_element_type=F32)
    each(nu, lambda off: gu_rs(off, mu).start())
    lax.fori_loop(0, 4, far_pass, 0)
    each(nu, lambda off: gu_rs(off, from_user(off)).wait_recv())
    total = gu_rows[0]
    for k in range(1, nu):
        total += gu_rows[k]
    gu[mine, :] = total
    each(ni, lambda off: gu_ag(off, mi).start())

    def item_pair(q):
        g = jnp.dot(uht[...], cf[:, rows(pair_i, q)], preferred_element_type=F32)
        g = g.T
        pack(g[:own_i], rs2_send.at[2 * q], own_i)
        pack(g[own_i:], rs2_send.at[2 * q + 1], own_i)

    def item_step(q, carry):
        item_pair(q)
        return carry

    lax.fori_loop(0, i_pairs, item_step, 0)
    each(ni, lambda off: gu_ag(off, from_item(off)).wait_recv())
    each(nu, lambda off: rs2(off).start())
    each(ni, lambda off: out_user(off, mi).start())
    sweep.begin(hessian(gu))

    def sweep_on(k, carry):
        sweep.block(k)
        return carry

    lax.fori_loop(0, d // PANEL, sweep_on, 0)
    sweep.end(hessian(gu))

    grad = unpack(rs2_send.at[mu], own_i)
    each(nu, lambda off: rs2(off).wait_recv())
    for off in range(1, nu):
        grad += unpack(rs2_recv.at[off], own_i)
    own = inat[rows(own_i, mu), :].astype(F32)
    grad = grad - REG * own
    new = own + jnp.dot(grad, inv_a[...], precision=EXACT, preferred_element_type=F32)
    i_new[...] = new.T
    each(nu, lambda off: out_item(off, mu).start())
    i_out[mu] = i_new[rows(wi, mu), :]

    gather_items.drain()
    gather_users.drain()
    gather_half.drain()

    def drain_item(off):
        gi_rs(off).wait_send()
        gi_ag(off, mi).wait_send()
        gu_ag(off, mi).wait_send()
        out_user(off, mi).wait_send()

    def drain_chip(k):
        halves(k).wait_send()

    def drain_user(off):
        rs2(off).wait_send()
        gu_rs(off, mu).wait_send()

    each(ni, drain_item)
    each(nk, lambda off: rs1(off).wait_send())
    each(nk, drain_chip, 0)
    for slot in range(len(HOPS) + 1):
        user_on(slot, core).wait_send()
        half_on(slot, core).wait_send()
    each(nu, drain_user)
    each(ni, lambda off: out_user(off, from_item(off)).wait_recv())
    each(nu, lambda off: out_item(off, from_user(off)).wait_recv())
    each(nu, lambda off: out_item(off, mu).wait_send())


def on_device(nu, ni, counts, user_factors, item_factors, alpha_scale):
    users, items = counts.shape
    d = user_factors.shape[1] * ni
    nk, slots = ni // 2, len(HOPS)
    wu, wi, own_u, own_i = d // ni, d // nu, users // ni, items // nu
    vmem = pl.BlockSpec(memory_space=pltpu.VMEM)
    spare, dma = pltpu.VMEM, pltpu.SemaphoreType.DMA
    u_out, i_out = pl.pallas_call(
        functools.partial(kernel, nu, ni),
        out_shape=(
            jax.ShapeDtypeStruct((wu, users), F32),
            jax.ShapeDtypeStruct((nu, wi, own_i), F32),
        ),
        in_specs=[
            pl.BlockSpec(memory_space=pltpu.SMEM), vmem, vmem, pl.BlockSpec(memory_space=pl.ANY),
        ],
        out_specs=(vmem, vmem),
        scratch_shapes=[
            spare((users, items), jnp.int32),
            spare((d, users), BF16), spare((d, items), BF16),
            spare((items, d), BF16),
            spare((users, items), BF16),
            spare((nk, own_u, d), F32), spare((nk, own_u, d), F32), spare((nk, own_u, d), F32),
            spare((nk, own_u + TILE, d), jnp.int16), spare((nk, own_u + TILE, d), jnp.int16),
            spare((d, d), F32), spare((ni, wu, d), F32), spare((d, d), F32),
            spare((users, d), BF16), spare((d, users), BF16), spare((d, own_u), F32),
            spare((nu, wu, d), F32), spare((d, d), F32),
            spare((nu, own_i + TILE, d), jnp.int16), spare((nu, own_i + TILE, d), jnp.int16),
            spare((d, own_i), F32),
            spare((d, d), F32), spare((d, LANES), F32), spare((PANEL, d), F32),
            dma((nk,)), dma((4, ni)), dma((4, ni)), dma((1, nk)), dma((1, nk)),
            dma((3, slots + 1)), dma((3, slots + 1)), dma((3, nu)), dma((3, nu)),
            dma((3, slots)), dma((3, slots)),
        ],
        compiler_params=pltpu.CompilerParams(
            collective_id=0, has_side_effects=True, vmem_limit_bytes=60 << 20
        ),
    )(alpha_scale, user_factors.T, item_factors.T, counts)

    def lay(u_ref, i_ref, u_to, i_to):
        u_to[...] = u_ref[...]
        for k in range(0, nu, 2):
            pair = jnp.concatenate([i_ref[k], i_ref[k + 1]], axis=1)
            i_to[:, k * own_i : (k + 2) * own_i] = pair

    u_new, i_new = pl.pallas_call(
        lay,
        out_shape=(jax.ShapeDtypeStruct((wu, users), F32), jax.ShapeDtypeStruct((wi, items), F32)),
        in_specs=[vmem, vmem],
        out_specs=(vmem, vmem),
    )(u_out, i_out)
    return u_new.T, i_new.T


def solution(mesh):
    in_specs = (P("user", "item"), P("user", "item"), P("item", "user"), P())
    out_specs = (P("user", "item"), P("item", "user"))
    return jax.shard_map(
        functools.partial(on_device, mesh.shape["user"], mesh.shape["item"]),
        mesh=mesh, in_specs=in_specs, out_specs=out_specs, check_vma=False,
    )
```

```python
import functools

import jax
import jax.numpy as jnp
from jax import lax
from jax.experimental import pallas as pl
from jax.experimental.pallas import tpu as pltpu
from jax.sharding import PartitionSpec as P

MESH = pl.DeviceIdType.MESH
EXACT = lax.Precision.HIGHEST
F32 = jnp.float32
BF16 = jnp.bfloat16
TN = (((0,), (0,)), ((), ()))
NT = (((1,), (1,)), ((), ()))
REG = 1.0
PANEL = 32
LANES = 128
TILE = 16
STEPS_BESIDE = 6
HOPS = (
    (1, 0, 0, 0, None, None),
    (-1, 0, 0, 0, None, None),
    (0, 1, 0, 0, None, None),
    (1, 0, -1, 0, 0, 0),
    (-1, 0, 1, 0, 1, 1),
    (1, 1, -1, 0, 0, 0),
    (-1, 1, 1, 0, 1, 1),
    (1, 0, 0, 1, None, 2),
    (-1, 0, 0, 1, None, 2),
)


def eye(n):
    return lax.broadcasted_iota(jnp.int32, (n, n), 0) == lax.broadcasted_iota(
        jnp.int32, (n, n), 1
    )


def scales(h):
    diagonal = jnp.where(eye(h.shape[0]), h, 0.0)
    return (
        lax.rsqrt(jnp.sum(diagonal, axis=0, keepdims=True)),
        lax.rsqrt(jnp.sum(diagonal, axis=1, keepdims=True)),
    )


def eliminations(d):
    sub = lax.broadcasted_iota(jnp.int32, (PANEL, LANES), 0)
    lane = lax.broadcasted_iota(jnp.int32, (PANEL, LANES), 1)

    def step(j):
        m = j % 8
        now = d["now"]
        if m == 0:
            d["cols"] = [jnp.broadcast_to(now[:, j + q : j + q + 1], (PANEL, LANES)) for q in range(8)]
        cols = d["cols"]
        c = cols[m]
        p = 1.0 / c[j : j + 1, :]
        for mm in range(m + 1, 8):
            y = cols[mm][j : j + 1, :] * p
            cols[mm] = jnp.where(sub == j, y, cols[mm] - c * y)
        y = jnp.where(lane[:1] == j, 1.0, now[j : j + 1, :]) * p
        d["now"] = jnp.where(sub == j, y, jnp.where(lane == j, 0.0, now) - c * y)

    return [functools.partial(step, j) for j in range(PANEL)]


class Sweep:
    def __init__(self, a_ref, u_ref, y_ref):
        self.a, self.u, self.y = a_ref, u_ref, y_ref
        self.n = a_ref.shape[0]

    def begin(self, h):
        s_row, s_col = scales(h)
        self.a[...] = h * s_row * s_col
        self.u[...] = jnp.zeros_like(self.u)
        self.y[...] = jnp.zeros_like(self.y)

    def update(self, k):
        ri = lax.broadcasted_iota(jnp.int32, (self.n, self.n), 0)
        inside = eye(self.n) & (ri >= (k - 1) * PANEL) & (ri < k * PANEL)
        return jnp.dot(self.u[:, :PANEL], self.y[...], precision=EXACT, preferred_element_type=F32) + jnp.where(inside, 2.0, 0.0)

    def block(self, k, beside=()):
        n = self.n
        rows = pl.ds(pl.multiple_of(k * PANEL, PANEL), PANEL)
        panel = self.a[rows, :] - jnp.dot(self.u[rows, :PANEL], self.y[...], precision=EXACT, preferred_element_type=F32)
        d = {"now": pltpu.roll(panel, lax.rem(n - k * PANEL, n), 1)[:, :LANES]}
        steps = eliminations(d)
        for work in beside[:-1]:
            work()
            for _ in range(STEPS_BESIDE):
                if steps:
                    steps.pop(0)()
        for step in steps:
            step()
        for work in beside[-1:]:
            work()
        self.a[...] = self.a[...] - self.update(k)
        lr = lax.broadcasted_iota(jnp.int32, (PANEL, n), 0)
        lc = lax.broadcasted_iota(jnp.int32, (PANEL, n), 1)
        y = panel - jnp.where(lc == lr + k * PANEL, 1.0, 0.0)
        self.y[...] = y
        self.u[:, :PANEL] = lax.dot_general(y, d["now"][:, :PANEL], TN, precision=EXACT, preferred_element_type=F32)

    def end(self, h):
        s_row, s_col = scales(h)
        self.a[...] = (self.update(self.n // PANEL) - self.a[...]) * s_row * s_col


def level(x):
    top = jnp.maximum(jnp.max(jnp.abs(x), axis=0, keepdims=True), 1e-30)
    return jnp.ceil(jnp.log2(top) - 14.99)


def pack(x, into, n):
    power = level(x)
    whole = jnp.clip(jnp.round(x * jnp.exp2(-power)), -32767.0, 32767.0)
    into[:n, :] = whole.astype(jnp.int32).astype(jnp.int16)
    into[n:, :] = jnp.broadcast_to(power, (TILE, x.shape[1])).astype(jnp.int32).astype(jnp.int16)


def unpack(ref, n):
    power = ref[n:, :].astype(jnp.int32).astype(F32)[:1]
    return ref[:n, :].astype(jnp.int32).astype(F32) * jnp.exp2(power)


def kernel(
    nu, ni,
    alpha_ref, u_in, i_in, counts_hbm, u_out, i_out,
    counts, ut, it, inat, cf,
    keep, sib_send, sib_recv, rs1_send, rs1_recv, gi_part, gi_recv, gi,
    uh, uht, u_new,
    gu_rows, gu,
    rs2_send, rs2_recv, i_new,
    inv_a, inv_u, inv_y,
    counts_sem, item_send, item_recv, line_send, line_recv, sib_sem, sib_done, user_send, user_recv,
    ring_send, ring_recv,
):
    mu, mi = lax.axis_index("user"), lax.axis_index("item")
    d, users = ut.shape
    items = it.shape[1]
    nk = ni // 2
    place, core = mi // 2, lax.rem(mi, 2)
    sibling = mi + 1 - 2 * core
    wu, wi = d // ni, d // nu
    own_u, own_i = users // ni, items // nu
    pair_u, pair_i = 2 * own_u, 2 * own_i
    i_pairs = nu // 2

    def rows(n, k):
        return pl.ds(pl.multiple_of(k * n, n), n)

    def item_peer(off):
        return lax.rem(mi + off, ni)

    def user_peer(off):
        return lax.rem(mu + off, nu)

    def after(off):
        return lax.rem(place + off, nk)

    def chip_at(along, across):
        y, z = lax.rem(place, 4), place // 4
        return 4 * lax.rem(z + across + 2, 2) + lax.rem(y + along + 4, 4)

    def group_at(along, across):
        x, z = mu // 2, lax.rem(mu, 2)
        return 2 * lax.rem(x + along + 4, 4) + lax.rem(z + across + 2, 2)

    def copy(src, dst, sent, landed, device):
        return pltpu.make_async_remote_copy(
            src_ref=src, dst_ref=dst, send_sem=sent, recv_sem=landed,
            device_id=device, device_id_type=MESH,
        )

    def over_item(kind, off, src, dst):
        return copy(src, dst, item_send.at[kind, off], item_recv.at[kind, off], (mu, item_peer(off)))

    def over_line(kind, off, src, dst):
        return copy(src, dst, line_send.at[kind, off], line_recv.at[kind, off], (mu, 2 * after(off) + core))

    def over_chip(kind, k, src, dst):
        return copy(src, dst, sib_sem.at[kind, k], sib_done.at[kind, k], (mu, sibling))

    def over_user(kind, off, src, dst):
        return copy(src, dst, user_send.at[kind, off], user_recv.at[kind, off], (user_peer(off), mi))

    class Gather:
        def __init__(self, kind, at, to, part):
            self.kind, self.at, self.to, self.part = kind, at, to, part

        def hop(self, slot):
            along, across, b_along, b_across, half, _ = HOPS[slot]
            ref = self.part(self.at(b_along, b_across), half)
            return copy(ref, ref, ring_send.at[self.kind, slot], ring_recv.at[self.kind, slot], self.to(self.at(along, across)))

        def landed(self, slot):
            along, across, b_along, b_across, half, _ = HOPS[slot]
            return self.part(self.at(b_along - along, b_across - across), half)

        def start(self):
            for slot in range(3):
                self.hop(slot).start()

        def arrived(self, slot):
            ref = self.landed(slot)
            copy(ref, ref, ring_send.at[self.kind, slot], ring_recv.at[self.kind, slot], self.to(self.at(0, 1))).wait_recv()
            for later in range(len(HOPS)):
                if HOPS[later][-1] == slot:
                    self.hop(later).start()

        def drain(self):
            for slot in range(len(HOPS)):
                self.hop(slot).wait_send()

    def item_part(k, half):
        if half is None:
            return it.at[rows(wi, k), :]
        return it.at[rows(wi // 2, 2 * k + half), :]

    def user_part_of(c):
        def part(k, half):
            if half is None:
                return ut.at[rows(wu, 2 * k + c), :]
            return ut.at[rows(wu, 2 * k + c), pl.ds(half * (users // 2), users // 2)]

        return part

    def half_part_of(c):
        def part(k, half):
            if half is None:
                return uh.at[rows(own_u, 2 * k + c), :]
            return uh.at[rows(own_u // 2, 4 * k + 2 * c + half), :]

        return part

    def same_core(k):
        return (mu, 2 * k + core)

    gather_items = Gather(0, group_at, lambda k: (k, mi), item_part)
    gather_users = Gather(1, chip_at, same_core, user_part_of(core))
    gather_half = Gather(2, chip_at, same_core, half_part_of(core))

    def passed_on(kind, slot, part_of, c):
        if slot == len(HOPS):
            ref = part_of(c)(place, None)
        else:
            along, across, b_along, b_across, half, _ = HOPS[slot]
            ref = part_of(c)(chip_at(b_along - along, b_across - across), half)
        return over_chip(kind, slot, ref, ref)

    def user_on(slot, c):
        return passed_on(0, slot, user_part_of, c)

    def half_on(slot, c):
        return passed_on(1, slot, half_part_of, c)

    own_slot = len(HOPS)

    def halves(k):
        return over_chip(2, k, sib_send.at[k], sib_recv.at[k])

    def rs1(off):
        return over_line(0, off, rs1_send.at[after(off)], rs1_recv.at[off])

    def gi_rs(off):
        return over_item(0, off, gi_part.at[rows(wu, item_peer(off)), :], gi_recv.at[off])

    def gi_ag(off, who):
        return over_item(1, off, gi.at[rows(wu, who), :], gi.at[rows(wu, who), :])

    def out_user(off, who):
        return over_item(
            2, off, u_new.at[rows(wu, item_peer(off)), :], u_out.at[:, rows(own_u, who)]
        )

    def gu_ag(off, who):
        return over_item(3, off, gu.at[rows(wu, who), :], gu.at[rows(wu, who), :])

    def rs2(off):
        return over_user(0, off, rs2_send.at[user_peer(off)], rs2_recv.at[off])

    def gu_rs(off, who):
        return over_user(1, off, gu_rows.at[who], gu_rows.at[who])

    def out_item(off, who):
        return over_user(2, off, i_new.at[rows(wi, user_peer(off)), :], i_out.at[who])

    def each(n, what, first=1):
        def step(off, carry):
            what(off)
            return carry

        lax.fori_loop(first, n, step, 0)

    def from_item(off):
        return lax.rem(mi + ni - off, ni)

    def from_user(off):
        return lax.rem(mu + nu - off, nu)

    def counts_copy(k):
        part = rows(pair_u, k)
        return pltpu.make_async_copy(
            counts_hbm.at[part, :], counts.at[part, :], counts_sem.at[k]
        )

    for k in range(nk):
        counts_copy(k).start()
    it[rows(wi, mu), :] = i_in[...]
    ut[rows(wu, mi), :] = u_in[...]

    barrier = pltpu.get_barrier_semaphore()
    each(ni, lambda off: pl.semaphore_signal(barrier, inc=1, device_id=(mu, item_peer(off)), device_id_type=MESH))
    each(nu, lambda off: pl.semaphore_signal(barrier, inc=1, device_id=(user_peer(off), mi), device_id_type=MESH))
    pl.semaphore_wait(barrier, ni + nu - 2)

    gather_items.start()
    gather_users.start()
    user_on(own_slot, core).start()
    for slot in range(2):
        gather_items.arrived(slot)
    for slot in range(2):
        gather_users.arrived(slot)
        user_on(slot, core).start()
    gather_items.arrived(2)
    gather_users.arrived(2)
    user_on(2, core).start()
    for slot in range(3, len(HOPS)):
        gather_items.arrived(slot)

    gi_part[...] = lax.dot_general(it[...], it[...], NT, preferred_element_type=F32)
    each(ni, lambda off: gi_rs(off).start())
    inat[...] = it[...].T

    for slot in range(3, len(HOPS)):
        gather_users.arrived(slot)
        user_on(slot, core).start()
    mine = rows(wu, mi)
    each(ni, lambda off: gi_rs(off).wait_recv())
    total = gi_part[mine, :]
    for off in range(1, ni):
        total += gi_recv[off]
    gi[mine, :] = total
    each(ni, lambda off: gi_ag(off, mi).start())

    for slot in range(len(HOPS) + 1):
        user_on(slot, 1 - core).wait_recv()
    for k in range(nk):
        counts_copy(k).wait()

    half_scale = alpha_ref[0] * 0.5

    def coefficients(half_left, part):
        step = 256

        def tile(t):
            cols = slice(t * step, (t + 1) * step)
            s = jnp.dot(half_left, it[:, cols], preferred_element_type=F32)
            a = counts[part, cols].astype(F32) * half_scale
            cf[part, cols] = ((a - 0.5) - (a + 0.5) * jnp.tanh(s)).astype(BF16)

        return [functools.partial(tile, t) for t in range(items // step)]

    def user_pair(k):
        part = rows(pair_u, k)

        def gradient():
            grad = jnp.dot(cf[part, :], inat[...], preferred_element_type=F32)
            lower, upper = grad[:own_u], grad[own_u:]
            keep[k] = jnp.where(core == 0, lower, upper)
            sib_send[k] = jnp.where(core == 0, upper, lower)

        return coefficients(ut[:, part].T * jnp.asarray(0.5, BF16), part) + [gradient]

    def on_to_owner(off):
        k = after(off)
        halves(k).wait_recv()
        pack(keep[k] + sib_recv[k], rs1_send.at[k], own_u)
        rs1(off).start()

    sweep = Sweep(inv_a, inv_u, inv_y)
    for work in user_pair(after(1)):
        work()
    halves(after(1)).start()
    each(ni, lambda off: gi_ag(off, from_item(off)).wait_recv())

    def hessian(gram):
        return 0.25 * gram[...] + jnp.where(eye(d), REG, 0.0)

    sweep.begin(hessian(gi))

    def first_pass(off, carry):
        sweep.block(off - 2, user_pair(after(off)))
        halves(after(off)).start()
        on_to_owner(off - 1)
        return carry

    lax.fori_loop(2, nk + 1, first_pass, 0)
    sweep.block(nk - 1)
    sweep.end(hessian(gi))

    halves(place).wait_recv()
    grad = keep[place] + sib_recv[place]
    for off in range(1, nk):
        rs1(off).wait_recv()
        grad += unpack(rs1_recv.at[off], own_u)
    own = ut[:, rows(own_u, mi)].T.astype(F32)
    grad = grad - REG * own
    new = own + jnp.dot(grad, inv_a[...], precision=EXACT, preferred_element_type=F32)
    uh[rows(own_u, mi), :] = new.astype(BF16)
    gather_half.start()
    half_on(own_slot, core).start()
    u_new[...] = new.T
    u_out[:, rows(own_u, mi)] = u_new[mine, :]

    def turn(k):
        part = rows(pair_u, k)
        uht[:, part] = uh[part, :].T

    def second_pass(k):
        part = rows(pair_u, k)
        half = uh[part, :]
        for work in coefficients(half * jnp.asarray(0.5, BF16), part):
            work()

    half_on(own_slot, 1 - core).wait_recv()
    second_pass(place)
    turn(place)
    for slot in range(3):
        gather_half.arrived(slot)
        half_on(slot, core).start()
    for slot in range(3):
        half_on(slot, 1 - core).wait_recv()

    def near(t, carry):
        k = chip_at(jnp.where(t == 0, -1, jnp.where(t == 1, 1, 0)), jnp.where(t == 2, 1, 0))
        second_pass(k)
        turn(k)
        return carry

    lax.fori_loop(0, 3, near, 0)
    for slot in range(3, len(HOPS)):
        gather_half.arrived(slot)
        half_on(slot, core).start()
    for slot in range(3, len(HOPS)):
        half_on(slot, 1 - core).wait_recv()

    def far(t):
        return chip_at(jnp.where(t < 2, 2, jnp.where(t == 2, 1, -1)), jnp.where(t == 0, 0, 1))

    def far_turn(t, carry):
        turn(far(t))
        return carry

    def far_pass(t, carry):
        second_pass(far(t))
        return carry

    lax.fori_loop(0, 4, far_turn, 0)
    gu_rows[mu] = jnp.dot(uht[mine, :], uh[...], preferred_element_type=F32)
    each(nu, lambda off: gu_rs(off, mu).start())
    each(ni, lambda off: out_user(off, mi).start())
    lax.fori_loop(0, 4, far_pass, 0)
    each(nu, lambda off: gu_rs(off, from_user(off)).wait_recv())
    total = gu_rows[0]
    for k in range(1, nu):
        total += gu_rows[k]
    gu[mine, :] = total
    each(ni, lambda off: gu_ag(off, mi).start())

    def item_pair(q):
        g = jnp.dot(uht[...], cf[:, rows(pair_i, q)], preferred_element_type=F32)
        g = g.T
        pack(g[:own_i], rs2_send.at[2 * q], own_i)
        pack(g[own_i:], rs2_send.at[2 * q + 1], own_i)

    def item_step(q, carry):
        item_pair(q)
        return carry

    lax.fori_loop(0, i_pairs, item_step, 0)
    each(ni, lambda off: gu_ag(off, from_item(off)).wait_recv())
    each(nu, lambda off: rs2(nu - off).start())
    sweep.begin(hessian(gu))

    def sweep_on(k, carry):
        sweep.block(k)
        return carry

    lax.fori_loop(0, d // PANEL, sweep_on, 0)
    sweep.end(hessian(gu))

    grad = unpack(rs2_send.at[mu], own_i)
    for off in range(nu - 1, 0, -1):
        rs2(off).wait_recv()
        grad += unpack(rs2_recv.at[off], own_i)
    own = inat[rows(own_i, mu), :].astype(F32)
    grad = grad - REG * own
    new = own + jnp.dot(grad, inv_a[...], precision=EXACT, preferred_element_type=F32)
    i_new[:, :own_i] = new.T
    each(nu, lambda off: out_item(off, mu).start())
    i_out[mu] = i_new[rows(wi, mu), :]

    gather_items.drain()
    gather_users.drain()
    gather_half.drain()

    def drain_item(off):
        gi_rs(off).wait_send()
        gi_ag(off, mi).wait_send()
        gu_ag(off, mi).wait_send()
        out_user(off, mi).wait_send()

    def drain_chip(k):
        halves(k).wait_send()

    def drain_user(off):
        rs2(off).wait_send()
        gu_rs(off, mu).wait_send()

    each(ni, drain_item)
    each(nk, lambda off: rs1(off).wait_send())
    each(nk, drain_chip, 0)
    for slot in range(len(HOPS) + 1):
        user_on(slot, core).wait_send()
        half_on(slot, core).wait_send()
    each(nu, drain_user)
    each(ni, lambda off: out_user(off, from_item(off)).wait_recv())
    each(nu, lambda off: out_item(off, from_user(off)).wait_recv())
    each(nu, lambda off: out_item(off, mu).wait_send())


def on_device(nu, ni, counts, user_factors, item_factors, alpha_scale):
    users, items = counts.shape
    d = user_factors.shape[1] * ni
    nk, slots = ni // 2, len(HOPS)
    wu, wi, own_u, own_i = d // ni, d // nu, users // ni, items // nu
    vmem = pl.BlockSpec(memory_space=pltpu.VMEM)
    spare, dma = pltpu.VMEM, pltpu.SemaphoreType.DMA
    u_out, i_out = pl.pallas_call(
        functools.partial(kernel, nu, ni),
        out_shape=(
            jax.ShapeDtypeStruct((wu, users), F32),
            jax.ShapeDtypeStruct((nu, wi, 2 * LANES), F32),
        ),
        in_specs=[
            pl.BlockSpec(memory_space=pltpu.SMEM), vmem, vmem, pl.BlockSpec(memory_space=pl.ANY),
        ],
        out_specs=(vmem, vmem),
        scratch_shapes=[
            spare((users, items), jnp.int32),
            spare((d, users), BF16), spare((d, items), BF16),
            spare((items, d), BF16),
            spare((users, items), BF16),
            spare((nk, own_u, d), F32), spare((nk, own_u, d), F32), spare((nk, own_u, d), F32),
            spare((nk, own_u + TILE, d), jnp.int16), spare((nk, own_u + TILE, d), jnp.int16),
            spare((d, d), F32), spare((ni, wu, d), F32), spare((d, d), F32),
            spare((users, d), BF16), spare((d, users), BF16), spare((d, own_u), F32),
            spare((nu, wu, d), F32), spare((d, d), F32),
            spare((nu, own_i + TILE, d), jnp.int16), spare((nu, own_i + TILE, d), jnp.int16),
            spare((d, 2 * LANES), F32),
            spare((d, d), F32), spare((d, LANES), F32), spare((PANEL, d), F32),
            dma((nk,)), dma((4, ni)), dma((4, ni)), dma((1, nk)), dma((1, nk)),
            dma((3, slots + 1)), dma((3, slots + 1)), dma((3, nu)), dma((3, nu)),
            dma((3, slots)), dma((3, slots)),
        ],
        compiler_params=pltpu.CompilerParams(
            collective_id=0, has_side_effects=True, vmem_limit_bytes=60 << 20
        ),
    )(alpha_scale, user_factors.T, item_factors.T, counts)

    def lay(u_ref, i_ref, u_to, i_to):
        u_to[...] = u_ref[...]
        for k in range(0, nu, 2):
            pair = jnp.concatenate([i_ref[k][:, :own_i], i_ref[k + 1][:, :own_i]], axis=1)
            i_to[:, k * own_i : (k + 2) * own_i] = pair

    u_new, i_new = pl.pallas_call(
        lay,
        out_shape=(jax.ShapeDtypeStruct((wu, users), F32), jax.ShapeDtypeStruct((wi, items), F32)),
        in_specs=[vmem, vmem],
        out_specs=(vmem, vmem),
    )(u_out, i_out)
    return u_new.T, i_new.T


def solution(mesh):
    in_specs = (P("user", "item"), P("user", "item"), P("item", "user"), P())
    out_specs = (P("user", "item"), P("item", "user"))
    return jax.shard_map(
        functools.partial(on_device, mesh.shape["user"], mesh.shape["item"]),
        mesh=mesh, in_specs=in_specs, out_specs=out_specs, check_vma=False,
    )
```

```python
import functools

import jax
import jax.numpy as jnp
from jax import lax
from jax.experimental import pallas as pl
from jax.experimental.pallas import tpu as pltpu
from jax.sharding import PartitionSpec as P

MESH = pl.DeviceIdType.MESH
EXACT = lax.Precision.HIGHEST
F32 = jnp.float32
BF16 = jnp.bfloat16
TN = (((0,), (0,)), ((), ()))
NT = (((1,), (1,)), ((), ()))
REG = 1.0
PANEL = 32
LANES = 128
TILE = 16
STEPS_BESIDE = 6
AHEAD = 4
HOPS = (
    (1, 0, 0, 0, None, None),
    (-1, 0, 0, 0, None, None),
    (0, 1, 0, 0, None, None),
    (1, 0, -1, 0, 0, 0),
    (-1, 0, 1, 0, 1, 1),
    (1, 1, -1, 0, 0, 0),
    (-1, 1, 1, 0, 1, 1),
    (1, 0, 0, 1, None, 2),
    (-1, 0, 0, 1, None, 2),
)


def eye(n):
    return lax.broadcasted_iota(jnp.int32, (n, n), 0) == lax.broadcasted_iota(
        jnp.int32, (n, n), 1
    )


def scales(h):
    diagonal = jnp.where(eye(h.shape[0]), h, 0.0)
    return (
        lax.rsqrt(jnp.sum(diagonal, axis=0, keepdims=True)),
        lax.rsqrt(jnp.sum(diagonal, axis=1, keepdims=True)),
    )


def eliminations(d):
    sub = lax.broadcasted_iota(jnp.int32, (PANEL, LANES), 0)
    lane = lax.broadcasted_iota(jnp.int32, (PANEL, LANES), 1)

    def step(j):
        m = j % 8
        now = d["now"]
        if m == 0:
            d["cols"] = [jnp.broadcast_to(now[:, j + q : j + q + 1], (PANEL, LANES)) for q in range(8)]
        cols = d["cols"]
        c = cols[m]
        p = 1.0 / c[j : j + 1, :]
        for mm in range(m + 1, 8):
            y = cols[mm][j : j + 1, :] * p
            cols[mm] = jnp.where(sub == j, y, cols[mm] - c * y)
        y = jnp.where(lane[:1] == j, 1.0, now[j : j + 1, :]) * p
        d["now"] = jnp.where(sub == j, y, jnp.where(lane == j, 0.0, now) - c * y)

    return [functools.partial(step, j) for j in range(PANEL)]


class Sweep:
    def __init__(self, a_ref, u_ref, y_ref):
        self.a, self.u, self.y = a_ref, u_ref, y_ref
        self.n = a_ref.shape[0]

    def begin(self, h):
        s_row, s_col = scales(h)
        self.a[...] = h * s_row * s_col
        self.u[...] = jnp.zeros_like(self.u)
        self.y[...] = jnp.zeros_like(self.y)

    def update(self, k):
        ri = lax.broadcasted_iota(jnp.int32, (self.n, self.n), 0)
        inside = eye(self.n) & (ri >= (k - 1) * PANEL) & (ri < k * PANEL)
        return jnp.dot(self.u[:, :PANEL], self.y[...], precision=EXACT, preferred_element_type=F32) + jnp.where(inside, 2.0, 0.0)

    def block(self, k, beside=()):
        n = self.n
        rows = pl.ds(pl.multiple_of(k * PANEL, PANEL), PANEL)
        panel = self.a[rows, :] - jnp.dot(self.u[rows, :PANEL], self.y[...], precision=EXACT, preferred_element_type=F32)
        d = {"now": pltpu.roll(panel, lax.rem(n - k * PANEL, n), 1)[:, :LANES]}
        steps = eliminations(d)
        for work in beside[:-1]:
            work()
            for _ in range(STEPS_BESIDE):
                if steps:
                    steps.pop(0)()
        for step in steps:
            step()
        for work in beside[-1:]:
            work()
        self.a[...] = self.a[...] - self.update(k)
        lr = lax.broadcasted_iota(jnp.int32, (PANEL, n), 0)
        lc = lax.broadcasted_iota(jnp.int32, (PANEL, n), 1)
        y = panel - jnp.where(lc == lr + k * PANEL, 1.0, 0.0)
        self.y[...] = y
        self.u[:, :PANEL] = lax.dot_general(y, d["now"][:, :PANEL], TN, precision=EXACT, preferred_element_type=F32)

    def end(self, h):
        s_row, s_col = scales(h)
        self.a[...] = (self.update(self.n // PANEL) - self.a[...]) * s_row * s_col


def level(x):
    top = jnp.maximum(jnp.max(jnp.abs(x), axis=0, keepdims=True), 1e-30)
    return jnp.ceil(jnp.log2(top) - 14.99)


def pack(x, into, n):
    power = level(x)
    whole = jnp.clip(jnp.round(x * jnp.exp2(-power)), -32767.0, 32767.0)
    into[:n, :] = whole.astype(jnp.int32).astype(jnp.int16)
    into[n:, :] = jnp.broadcast_to(power, (TILE, x.shape[1])).astype(jnp.int32).astype(jnp.int16)


def unpack(ref, n):
    power = ref[n:, :].astype(jnp.int32).astype(F32)[:1]
    return ref[:n, :].astype(jnp.int32).astype(F32) * jnp.exp2(power)


def kernel(
    nu, ni,
    alpha_ref, u_in, i_in, counts_hbm, u_out, i_out,
    counts, ut, it, inat, cf,
    keep, sib_send, sib_recv, rs1_send, rs1_recv, gi_part, gi_recv, gi,
    uh, uht, u_new,
    gu_rows, gu,
    rs2_send, rs2_recv, i_new,
    inv_a, inv_u, inv_y,
    counts_sem, item_send, item_recv, line_send, line_recv, sib_sem, sib_done, user_send, user_recv,
    ring_send, ring_recv,
):
    mu, mi = lax.axis_index("user"), lax.axis_index("item")
    d, users = ut.shape
    items = it.shape[1]
    nk = ni // 2
    place, core = mi // 2, lax.rem(mi, 2)
    sibling = mi + 1 - 2 * core
    wu, wi = d // ni, d // nu
    own_u, own_i = users // ni, items // nu
    pair_u, pair_i = 2 * own_u, 2 * own_i
    i_pairs = nu // 2

    def rows(n, k):
        return pl.ds(pl.multiple_of(k * n, n), n)

    def item_peer(off):
        return lax.rem(mi + off, ni)

    def user_peer(off):
        return lax.rem(mu + off, nu)

    def after(off):
        return lax.rem(place + off, nk)

    def chip_at(along, across):
        y, z = lax.rem(place, 4), place // 4
        return 4 * lax.rem(z + across + 2, 2) + lax.rem(y + along + 4, 4)

    def group_at(along, across):
        x, z = mu // 2, lax.rem(mu, 2)
        return 2 * lax.rem(x + along + 4, 4) + lax.rem(z + across + 2, 2)

    def copy(src, dst, sent, landed, device):
        return pltpu.make_async_remote_copy(
            src_ref=src, dst_ref=dst, send_sem=sent, recv_sem=landed,
            device_id=device, device_id_type=MESH,
        )

    def over_item(kind, off, src, dst):
        return copy(src, dst, item_send.at[kind, off], item_recv.at[kind, off], (mu, item_peer(off)))

    def over_line(kind, off, src, dst):
        return copy(src, dst, line_send.at[kind, off], line_recv.at[kind, off], (mu, 2 * after(off) + core))

    def over_chip(kind, k, src, dst):
        return copy(src, dst, sib_sem.at[kind, k], sib_done.at[kind, k], (mu, sibling))

    def over_user(kind, off, src, dst):
        return copy(src, dst, user_send.at[kind, off], user_recv.at[kind, off], (user_peer(off), mi))

    class Gather:
        def __init__(self, kind, at, to, part):
            self.kind, self.at, self.to, self.part = kind, at, to, part

        def hop(self, slot):
            along, across, b_along, b_across, half, _ = HOPS[slot]
            ref = self.part(self.at(b_along, b_across), half)
            return copy(ref, ref, ring_send.at[self.kind, slot], ring_recv.at[self.kind, slot], self.to(self.at(along, across)))

        def landed(self, slot):
            along, across, b_along, b_across, half, _ = HOPS[slot]
            return self.part(self.at(b_along - along, b_across - across), half)

        def start(self):
            for slot in range(3):
                self.hop(slot).start()

        def arrived(self, slot):
            ref = self.landed(slot)
            copy(ref, ref, ring_send.at[self.kind, slot], ring_recv.at[self.kind, slot], self.to(self.at(0, 1))).wait_recv()
            for later in range(len(HOPS)):
                if HOPS[later][-1] == slot:
                    self.hop(later).start()

        def drain(self):
            for slot in range(len(HOPS)):
                self.hop(slot).wait_send()

    def item_part(k, half):
        if half is None:
            return it.at[rows(wi, k), :]
        return it.at[rows(wi // 2, 2 * k + half), :]

    def user_part_of(c):
        def part(k, half):
            if half is None:
                return ut.at[rows(wu, 2 * k + c), :]
            return ut.at[rows(wu, 2 * k + c), pl.ds(half * (users // 2), users // 2)]

        return part

    def half_part_of(c):
        def part(k, half):
            if half is None:
                return uh.at[rows(own_u, 2 * k + c), :]
            return uh.at[rows(own_u // 2, 4 * k + 2 * c + half), :]

        return part

    def same_core(k):
        return (mu, 2 * k + core)

    gather_items = Gather(0, group_at, lambda k: (k, mi), item_part)
    gather_users = Gather(1, chip_at, same_core, user_part_of(core))
    gather_half = Gather(2, chip_at, same_core, half_part_of(core))

    def passed_on(kind, slot, part_of, c):
        if slot == len(HOPS):
            ref = part_of(c)(place, None)
        else:
            along, across, b_along, b_across, half, _ = HOPS[slot]
            ref = part_of(c)(chip_at(b_along - along, b_across - across), half)
        return over_chip(kind, slot, ref, ref)

    def user_on(slot, c):
        return passed_on(0, slot, user_part_of, c)

    def half_on(slot, c):
        return passed_on(1, slot, half_part_of, c)

    own_slot = len(HOPS)

    def halves(k):
        return over_chip(2, k, sib_send.at[k], sib_recv.at[k])

    def rs1(off):
        return over_line(0, off, rs1_send.at[after(off)], rs1_recv.at[off])

    def gi_rs(off):
        return over_item(0, off, gi_part.at[rows(wu, item_peer(off)), :], gi_recv.at[off])

    def gi_ag(off, who):
        return over_item(1, off, gi.at[rows(wu, who), :], gi.at[rows(wu, who), :])

    def out_user(off, who):
        return over_item(
            2, off, u_new.at[rows(wu, item_peer(off)), :], u_out.at[:, rows(own_u, who)]
        )

    def gu_ag(off, who):
        return over_item(3, off, gu.at[rows(wu, who), :], gu.at[rows(wu, who), :])

    def rs2(off):
        return over_user(0, off, rs2_send.at[user_peer(off)], rs2_recv.at[off])

    def gu_rs(off, who):
        return over_user(1, off, gu_rows.at[who], gu_rows.at[who])

    def out_item(off, who):
        return over_user(2, off, i_new.at[rows(wi, user_peer(off)), :], i_out.at[who])

    def each(n, what, first=1):
        def step(off, carry):
            what(off)
            return carry

        lax.fori_loop(first, n, step, 0)

    def from_item(off):
        return lax.rem(mi + ni - off, ni)

    def from_user(off):
        return lax.rem(mu + nu - off, nu)

    def counts_copy(k):
        part = rows(pair_u, k)
        return pltpu.make_async_copy(
            counts_hbm.at[part, :], counts.at[part, :], counts_sem.at[k]
        )

    for k in range(nk):
        counts_copy(k).start()
    it[rows(wi, mu), :] = i_in[...]
    ut[rows(wu, mi), :] = u_in[...]

    barrier = pltpu.get_barrier_semaphore()
    each(ni, lambda off: pl.semaphore_signal(barrier, inc=1, device_id=(mu, item_peer(off)), device_id_type=MESH))
    each(nu, lambda off: pl.semaphore_signal(barrier, inc=1, device_id=(user_peer(off), mi), device_id_type=MESH))
    pl.semaphore_wait(barrier, ni + nu - 2)

    gather_items.start()
    gather_users.start()
    user_on(own_slot, core).start()
    for slot in range(2):
        gather_items.arrived(slot)
    for slot in range(2):
        gather_users.arrived(slot)
        user_on(slot, core).start()
    gather_items.arrived(2)
    gather_users.arrived(2)
    user_on(2, core).start()
    for slot in range(3, len(HOPS)):
        gather_items.arrived(slot)

    gi_part[...] = lax.dot_general(it[...], it[...], NT, preferred_element_type=F32)
    each(ni, lambda off: gi_rs(off).start())
    inat[...] = it[...].T

    for slot in range(3, len(HOPS)):
        gather_users.arrived(slot)
        user_on(slot, core).start()
    mine = rows(wu, mi)
    each(ni, lambda off: gi_rs(off).wait_recv())
    total = gi_part[mine, :]
    for off in range(1, ni):
        total += gi_recv[off]
    gi[mine, :] = total
    each(ni, lambda off: gi_ag(off, mi).start())

    for slot in range(len(HOPS) + 1):
        user_on(slot, 1 - core).wait_recv()
    for k in range(nk):
        counts_copy(k).wait()

    half_scale = alpha_ref[0] * 0.5

    def coefficients(half_left, part):
        step = 256

        def tile(t):
            cols = slice(t * step, (t + 1) * step)
            s = jnp.dot(half_left, it[:, cols], preferred_element_type=F32)
            a = counts[part, cols].astype(F32) * half_scale
            cf[part, cols] = ((a - 0.5) - (a + 0.5) * jnp.tanh(s)).astype(BF16)

        return [functools.partial(tile, t) for t in range(items // step)]

    def user_pair(k):
        part = rows(pair_u, k)

        def gradient():
            grad = jnp.dot(cf[part, :], inat[...], preferred_element_type=F32)
            lower, upper = grad[:own_u], grad[own_u:]
            keep[k] = jnp.where(core == 0, lower, upper)
            sib_send[k] = jnp.where(core == 0, upper, lower)

        return coefficients(ut[:, part].T * jnp.asarray(0.5, BF16), part) + [gradient]

    def on_to_owner(off):
        k = after(off)
        halves(k).wait_recv()
        pack(keep[k] + sib_recv[k], rs1_send.at[k], own_u)
        rs1(off).start()

    sweep = Sweep(inv_a, inv_u, inv_y)
    def plain_pass(off):
        for work in user_pair(after(off)):
            work()
        halves(after(off)).start()

    def plain_step(off, carry):
        plain_pass(off)
        on_to_owner(off - 1)
        return carry

    plain_pass(1)
    lax.fori_loop(2, AHEAD + 1, plain_step, 0)
    each(ni, lambda off: gi_ag(off, from_item(off)).wait_recv())

    def hessian(gram):
        return 0.25 * gram[...] + jnp.where(eye(d), REG, 0.0)

    sweep.begin(hessian(gi))

    def first_pass(off, carry):
        sweep.block(off - 1 - AHEAD, user_pair(after(off)))
        halves(after(off)).start()
        on_to_owner(off - 1)
        return carry

    def sweep_on(k, carry):
        sweep.block(k)
        return carry

    lax.fori_loop(AHEAD + 1, nk + 1, first_pass, 0)
    lax.fori_loop(nk - AHEAD, nk, sweep_on, 0)
    sweep.end(hessian(gi))

    halves(place).wait_recv()
    grad = keep[place] + sib_recv[place]
    for off in range(1, nk):
        rs1(off).wait_recv()
        grad += unpack(rs1_recv.at[off], own_u)
    own = ut[:, rows(own_u, mi)].T.astype(F32)
    grad = grad - REG * own
    new = own + jnp.dot(grad, inv_a[...], precision=EXACT, preferred_element_type=F32)
    uh[rows(own_u, mi), :] = new.astype(BF16)
    gather_half.start()
    half_on(own_slot, core).start()
    u_new[...] = new.T
    u_out[:, rows(own_u, mi)] = u_new[mine, :]

    def turn(k):
        part = rows(pair_u, k)
        uht[:, part] = uh[part, :].T

    def second_pass(k):
        part = rows(pair_u, k)
        half = uh[part, :]
        for work in coefficients(half * jnp.asarray(0.5, BF16), part):
            work()

    half_on(own_slot, 1 - core).wait_recv()
    second_pass(place)
    turn(place)
    for slot in range(3):
        gather_half.arrived(slot)
        half_on(slot, core).start()
    for slot in range(3):
        half_on(slot, 1 - core).wait_recv()

    def near(t, carry):
        k = chip_at(jnp.where(t == 0, -1, jnp.where(t == 1, 1, 0)), jnp.where(t == 2, 1, 0))
        second_pass(k)
        turn(k)
        return carry

    lax.fori_loop(0, 3, near, 0)
    for slot in range(3, len(HOPS)):
        gather_half.arrived(slot)
        half_on(slot, core).start()
    for slot in range(3, len(HOPS)):
        half_on(slot, 1 - core).wait_recv()

    def far(t):
        return chip_at(jnp.where(t < 2, 2, jnp.where(t == 2, 1, -1)), jnp.where(t == 0, 0, 1))

    def far_turn(t, carry):
        turn(far(t))
        return carry

    def far_pass(t, carry):
        second_pass(far(t))
        return carry

    lax.fori_loop(0, 4, far_turn, 0)
    gu_rows[mu] = jnp.dot(uht[mine, :], uh[...], preferred_element_type=F32)
    each(nu, lambda off: gu_rs(off, mu).start())
    each(ni, lambda off: out_user(off, mi).start())
    lax.fori_loop(0, 4, far_pass, 0)
    each(nu, lambda off: gu_rs(off, from_user(off)).wait_recv())
    total = gu_rows[0]
    for k in range(1, nu):
        total += gu_rows[k]
    gu[mine, :] = total
    each(ni, lambda off: gu_ag(off, mi).start())

    def item_pair(q):
        g = jnp.dot(uht[...], cf[:, rows(pair_i, q)], preferred_element_type=F32)
        g = g.T
        pack(g[:own_i], rs2_send.at[2 * q], own_i)
        pack(g[own_i:], rs2_send.at[2 * q + 1], own_i)

    def item_step(q, carry):
        item_pair(q)
        return carry

    lax.fori_loop(0, i_pairs, item_step, 0)
    each(ni, lambda off: gu_ag(off, from_item(off)).wait_recv())
    each(nu, lambda off: rs2(nu - off).start())
    sweep.begin(hessian(gu))

    lax.fori_loop(0, d // PANEL, sweep_on, 0)
    sweep.end(hessian(gu))

    grad = unpack(rs2_send.at[mu], own_i)
    for off in range(nu - 1, 0, -1):
        rs2(off).wait_recv()
        grad += unpack(rs2_recv.at[off], own_i)
    own = inat[rows(own_i, mu), :].astype(F32)
    grad = grad - REG * own
    new = own + jnp.dot(grad, inv_a[...], precision=EXACT, preferred_element_type=F32)
    i_new[:, :own_i] = new.T
    each(nu, lambda off: out_item(off, mu).start())
    i_out[mu] = i_new[rows(wi, mu), :]

    gather_items.drain()
    gather_users.drain()
    gather_half.drain()

    def drain_item(off):
        gi_rs(off).wait_send()
        gi_ag(off, mi).wait_send()
        gu_ag(off, mi).wait_send()
        out_user(off, mi).wait_send()

    def drain_chip(k):
        halves(k).wait_send()

    def drain_user(off):
        rs2(off).wait_send()
        gu_rs(off, mu).wait_send()

    each(ni, drain_item)
    each(nk, lambda off: rs1(off).wait_send())
    each(nk, drain_chip, 0)
    for slot in range(len(HOPS) + 1):
        user_on(slot, core).wait_send()
        half_on(slot, core).wait_send()
    each(nu, drain_user)
    each(ni, lambda off: out_user(off, from_item(off)).wait_recv())
    each(nu, lambda off: out_item(off, from_user(off)).wait_recv())
    each(nu, lambda off: out_item(off, mu).wait_send())


def on_device(nu, ni, counts, user_factors, item_factors, alpha_scale):
    users, items = counts.shape
    d = user_factors.shape[1] * ni
    nk, slots = ni // 2, len(HOPS)
    wu, wi, own_u, own_i = d // ni, d // nu, users // ni, items // nu
    vmem = pl.BlockSpec(memory_space=pltpu.VMEM)
    spare, dma = pltpu.VMEM, pltpu.SemaphoreType.DMA
    u_out, i_out = pl.pallas_call(
        functools.partial(kernel, nu, ni),
        out_shape=(
            jax.ShapeDtypeStruct((wu, users), F32),
            jax.ShapeDtypeStruct((nu, wi, 2 * LANES), F32),
        ),
        in_specs=[
            pl.BlockSpec(memory_space=pltpu.SMEM), vmem, vmem, pl.BlockSpec(memory_space=pl.ANY),
        ],
        out_specs=(vmem, vmem),
        scratch_shapes=[
            spare((users, items), jnp.int32),
            spare((d, users), BF16), spare((d, items), BF16),
            spare((items, d), BF16),
            spare((users, items), BF16),
            spare((nk, own_u, d), F32), spare((nk, own_u, d), F32), spare((nk, own_u, d), F32),
            spare((nk, own_u + TILE, d), jnp.int16), spare((nk, own_u + TILE, d), jnp.int16),
            spare((d, d), F32), spare((ni, wu, d), F32), spare((d, d), F32),
            spare((users, d), BF16), spare((d, users), BF16), spare((d, own_u), F32),
            spare((nu, wu, d), F32), spare((d, d), F32),
            spare((nu, own_i + TILE, d), jnp.int16), spare((nu, own_i + TILE, d), jnp.int16),
            spare((d, 2 * LANES), F32),
            spare((d, d), F32), spare((d, LANES), F32), spare((PANEL, d), F32),
            dma((nk,)), dma((4, ni)), dma((4, ni)), dma((1, nk)), dma((1, nk)),
            dma((3, slots + 1)), dma((3, slots + 1)), dma((3, nu)), dma((3, nu)),
            dma((3, slots)), dma((3, slots)),
        ],
        compiler_params=pltpu.CompilerParams(
            collective_id=0, has_side_effects=True, vmem_limit_bytes=60 << 20
        ),
    )(alpha_scale, user_factors.T, item_factors.T, counts)

    def lay(u_ref, i_ref, u_to, i_to):
        u_to[...] = u_ref[...]
        for k in range(0, nu, 2):
            pair = jnp.concatenate([i_ref[k][:, :own_i], i_ref[k + 1][:, :own_i]], axis=1)
            i_to[:, k * own_i : (k + 2) * own_i] = pair

    u_new, i_new = pl.pallas_call(
        lay,
        out_shape=(jax.ShapeDtypeStruct((wu, users), F32), jax.ShapeDtypeStruct((wi, items), F32)),
        in_specs=[vmem, vmem],
        out_specs=(vmem, vmem),
    )(u_out, i_out)
    return u_new.T, i_new.T


def solution(mesh):
    in_specs = (P("user", "item"), P("user", "item"), P("item", "user"), P())
    out_specs = (P("user", "item"), P("item", "user"))
    return jax.shard_map(
        functools.partial(on_device, mesh.shape["user"], mesh.shape["item"]),
        mesh=mesh, in_specs=in_specs, out_specs=out_specs, check_vma=False,
    )
```

```python
import functools

import jax
import jax.numpy as jnp
from jax import lax
from jax.experimental import pallas as pl
from jax.experimental.pallas import tpu as pltpu
from jax.sharding import PartitionSpec as P

MESH = pl.DeviceIdType.MESH
EXACT = lax.Precision.HIGHEST
F32 = jnp.float32
BF16 = jnp.bfloat16
TN = (((0,), (0,)), ((), ()))
NT = (((1,), (1,)), ((), ()))
REG = 1.0
PANEL = 32
LANES = 128
TILE = 16
STEPS_BESIDE = 6
AHEAD = 5
HOPS = (
    (1, 0, 0, 0, None, None),
    (-1, 0, 0, 0, None, None),
    (0, 1, 0, 0, None, None),
    (1, 0, -1, 0, 0, 0),
    (-1, 0, 1, 0, 1, 1),
    (1, 1, -1, 0, 0, 0),
    (-1, 1, 1, 0, 1, 1),
    (1, 0, 0, 1, None, 2),
    (-1, 0, 0, 1, None, 2),
)


def eye(n):
    return lax.broadcasted_iota(jnp.int32, (n, n), 0) == lax.broadcasted_iota(
        jnp.int32, (n, n), 1
    )


def scales(h):
    diagonal = jnp.where(eye(h.shape[0]), h, 0.0)
    return (
        lax.rsqrt(jnp.sum(diagonal, axis=0, keepdims=True)),
        lax.rsqrt(jnp.sum(diagonal, axis=1, keepdims=True)),
    )


def eliminations(d):
    sub = lax.broadcasted_iota(jnp.int32, (PANEL, LANES), 0)
    lane = lax.broadcasted_iota(jnp.int32, (PANEL, LANES), 1)

    def step(j):
        m = j % 8
        now = d["now"]
        if m == 0:
            d["cols"] = [jnp.broadcast_to(now[:, j + q : j + q + 1], (PANEL, LANES)) for q in range(8)]
        cols = d["cols"]
        c = cols[m]
        p = 1.0 / c[j : j + 1, :]
        for mm in range(m + 1, 8):
            y = cols[mm][j : j + 1, :] * p
            cols[mm] = jnp.where(sub == j, y, cols[mm] - c * y)
        y = jnp.where(lane[:1] == j, 1.0, now[j : j + 1, :]) * p
        d["now"] = jnp.where(sub == j, y, jnp.where(lane == j, 0.0, now) - c * y)

    return [functools.partial(step, j) for j in range(PANEL)]


class Sweep:
    def __init__(self, a_ref, u_ref, y_ref):
        self.a, self.u, self.y = a_ref, u_ref, y_ref
        self.n = a_ref.shape[0]

    def begin(self, h):
        s_row, s_col = scales(h)
        self.a[...] = h * s_row * s_col
        self.u[...] = jnp.zeros_like(self.u)
        self.y[...] = jnp.zeros_like(self.y)

    def update(self, k):
        ri = lax.broadcasted_iota(jnp.int32, (self.n, self.n), 0)
        inside = eye(self.n) & (ri >= (k - 1) * PANEL) & (ri < k * PANEL)
        return jnp.dot(self.u[:, :PANEL], self.y[...], precision=EXACT, preferred_element_type=F32) + jnp.where(inside, 2.0, 0.0)

    def block(self, k, beside=()):
        n = self.n
        rows = pl.ds(pl.multiple_of(k * PANEL, PANEL), PANEL)
        panel = self.a[rows, :] - jnp.dot(self.u[rows, :PANEL], self.y[...], precision=EXACT, preferred_element_type=F32)
        d = {"now": pltpu.roll(panel, lax.rem(n - k * PANEL, n), 1)[:, :LANES]}
        steps = eliminations(d)
        for work in beside[:-1]:
            work()
            for _ in range(STEPS_BESIDE):
                if steps:
                    steps.pop(0)()
        for step in steps:
            step()
        for work in beside[-1:]:
            work()
        self.a[...] = self.a[...] - self.update(k)
        lr = lax.broadcasted_iota(jnp.int32, (PANEL, n), 0)
        lc = lax.broadcasted_iota(jnp.int32, (PANEL, n), 1)
        y = panel - jnp.where(lc == lr + k * PANEL, 1.0, 0.0)
        self.y[...] = y
        self.u[:, :PANEL] = lax.dot_general(y, d["now"][:, :PANEL], TN, precision=EXACT, preferred_element_type=F32)

    def end(self, h):
        s_row, s_col = scales(h)
        self.a[...] = (self.update(self.n // PANEL) - self.a[...]) * s_row * s_col


def level(x):
    top = jnp.maximum(jnp.max(jnp.abs(x), axis=0, keepdims=True), 1e-30)
    return jnp.ceil(jnp.log2(top) - 14.99)


def pack(x, into, n):
    power = level(x)
    whole = jnp.clip(jnp.round(x * jnp.exp2(-power)), -32767.0, 32767.0)
    into[:n, :] = whole.astype(jnp.int32).astype(jnp.int16)
    into[n:, :] = jnp.broadcast_to(power, (TILE, x.shape[1])).astype(jnp.int32).astype(jnp.int16)


def unpack(ref, n):
    power = ref[n:, :].astype(jnp.int32).astype(F32)[:1]
    return ref[:n, :].astype(jnp.int32).astype(F32) * jnp.exp2(power)


def kernel(
    nu, ni,
    alpha_ref, u_in, i_in, counts_hbm, u_out, i_out,
    counts, ut, it, inat, cf,
    keep, sib_send, sib_recv, rs1_send, rs1_recv, gi_part, gi_recv, gi,
    uh, uht, u_new,
    gu_rows, gu,
    rs2_send, rs2_recv, i_new,
    inv_a, inv_u, inv_y,
    counts_sem, item_send, item_recv, line_send, line_recv, sib_sem, sib_done, user_send, user_recv,
    ring_send, ring_recv,
):
    mu, mi = lax.axis_index("user"), lax.axis_index("item")
    d, users = ut.shape
    items = it.shape[1]
    nk = ni // 2
    place, core = mi // 2, lax.rem(mi, 2)
    sibling = mi + 1 - 2 * core
    wu, wi = d // ni, d // nu
    own_u, own_i = users // ni, items // nu
    pair_u, pair_i = 2 * own_u, 2 * own_i
    i_pairs = nu // 2

    def rows(n, k):
        return pl.ds(pl.multiple_of(k * n, n), n)

    def item_peer(off):
        return lax.rem(mi + off, ni)

    def user_peer(off):
        return lax.rem(mu + off, nu)

    def after(off):
        return lax.rem(place + off, nk)

    def chip_at(along, across):
        y, z = lax.rem(place, 4), place // 4
        return 4 * lax.rem(z + across + 2, 2) + lax.rem(y + along + 4, 4)

    def group_at(along, across):
        x, z = mu // 2, lax.rem(mu, 2)
        return 2 * lax.rem(x + along + 4, 4) + lax.rem(z + across + 2, 2)

    def copy(src, dst, sent, landed, device):
        return pltpu.make_async_remote_copy(
            src_ref=src, dst_ref=dst, send_sem=sent, recv_sem=landed,
            device_id=device, device_id_type=MESH,
        )

    def over_item(kind, off, src, dst):
        return copy(src, dst, item_send.at[kind, off], item_recv.at[kind, off], (mu, item_peer(off)))

    def over_line(kind, off, src, dst):
        return copy(src, dst, line_send.at[kind, off], line_recv.at[kind, off], (mu, 2 * after(off) + core))

    def over_chip(kind, k, src, dst):
        return copy(src, dst, sib_sem.at[kind, k], sib_done.at[kind, k], (mu, sibling))

    def over_user(kind, off, src, dst):
        return copy(src, dst, user_send.at[kind, off], user_recv.at[kind, off], (user_peer(off), mi))

    class Gather:
        def __init__(self, kind, at, to, part):
            self.kind, self.at, self.to, self.part = kind, at, to, part

        def hop(self, slot):
            along, across, b_along, b_across, half, _ = HOPS[slot]
            ref = self.part(self.at(b_along, b_across), half)
            return copy(ref, ref, ring_send.at[self.kind, slot], ring_recv.at[self.kind, slot], self.to(self.at(along, across)))

        def landed(self, slot):
            along, across, b_along, b_across, half, _ = HOPS[slot]
            return self.part(self.at(b_along - along, b_across - across), half)

        def start(self):
            for slot in range(3):
                self.hop(slot).start()

        def arrived(self, slot):
            ref = self.landed(slot)
            copy(ref, ref, ring_send.at[self.kind, slot], ring_recv.at[self.kind, slot], self.to(self.at(0, 1))).wait_recv()
            for later in range(len(HOPS)):
                if HOPS[later][-1] == slot:
                    self.hop(later).start()

        def drain(self):
            for slot in range(len(HOPS)):
                self.hop(slot).wait_send()

    def item_part(k, half):
        if half is None:
            return it.at[rows(wi, k), :]
        return it.at[rows(wi // 2, 2 * k + half), :]

    def user_part_of(c):
        def part(k, half):
            if half is None:
                return ut.at[rows(wu, 2 * k + c), :]
            return ut.at[rows(wu, 2 * k + c), pl.ds(half * (users // 2), users // 2)]

        return part

    def half_part_of(c):
        def part(k, half):
            if half is None:
                return uh.at[rows(own_u, 2 * k + c), :]
            return uh.at[rows(own_u // 2, 4 * k + 2 * c + half), :]

        return part

    def same_core(k):
        return (mu, 2 * k + core)

    gather_items = Gather(0, group_at, lambda k: (k, mi), item_part)
    gather_users = Gather(1, chip_at, same_core, user_part_of(core))
    gather_half = Gather(2, chip_at, same_core, half_part_of(core))

    def passed_on(kind, slot, part_of, c):
        if slot == len(HOPS):
            ref = part_of(c)(place, None)
        else:
            along, across, b_along, b_across, half, _ = HOPS[slot]
            ref = part_of(c)(chip_at(b_along - along, b_across - across), half)
        return over_chip(kind, slot, ref, ref)

    def user_on(slot, c):
        return passed_on(0, slot, user_part_of, c)

    def half_on(slot, c):
        return passed_on(1, slot, half_part_of, c)

    own_slot = len(HOPS)

    def halves(k):
        return over_chip(2, k, sib_send.at[k], sib_recv.at[k])

    def rs1(off):
        return over_line(0, off, rs1_send.at[after(off)], rs1_recv.at[off])

    def gi_rs(off):
        return over_item(0, off, gi_part.at[rows(wu, item_peer(off)), :], gi_recv.at[off])

    def gi_ag(off, who):
        return over_item(1, off, gi.at[rows(wu, who), :], gi.at[rows(wu, who), :])

    def out_user(off, who):
        return over_item(
            2, off, u_new.at[rows(wu, item_peer(off)), :], u_out.at[:, rows(own_u, who)]
        )

    def gu_ag(off, who):
        return over_item(3, off, gu.at[rows(wu, who), :], gu.at[rows(wu, who), :])

    def rs2(off):
        return over_user(0, off, rs2_send.at[user_peer(off)], rs2_recv.at[off])

    def gu_rs(off, who):
        return over_user(1, off, gu_rows.at[who], gu_rows.at[who])

    def out_item(off, who):
        return over_user(2, off, i_new.at[rows(wi, user_peer(off)), :], i_out.at[who])

    def each(n, what, first=1):
        def step(off, carry):
            what(off)
            return carry

        lax.fori_loop(first, n, step, 0)

    def from_item(off):
        return lax.rem(mi + ni - off, ni)

    def from_user(off):
        return lax.rem(mu + nu - off, nu)

    def counts_copy(k):
        part = rows(pair_u, k)
        return pltpu.make_async_copy(
            counts_hbm.at[part, :], counts.at[part, :], counts_sem.at[k]
        )

    for k in range(nk):
        counts_copy(k).start()
    it[rows(wi, mu), :] = i_in[...]
    ut[rows(wu, mi), :] = u_in[...]

    barrier = pltpu.get_barrier_semaphore()
    each(ni, lambda off: pl.semaphore_signal(barrier, inc=1, device_id=(mu, item_peer(off)), device_id_type=MESH))
    each(nu, lambda off: pl.semaphore_signal(barrier, inc=1, device_id=(user_peer(off), mi), device_id_type=MESH))
    pl.semaphore_wait(barrier, ni + nu - 2)

    gather_items.start()
    gather_users.start()
    user_on(own_slot, core).start()
    for slot in range(2):
        gather_items.arrived(slot)
    for slot in range(2):
        gather_users.arrived(slot)
        user_on(slot, core).start()
    gather_items.arrived(2)
    gather_users.arrived(2)
    user_on(2, core).start()
    for slot in range(3, len(HOPS)):
        gather_items.arrived(slot)

    gi_part[...] = lax.dot_general(it[...], it[...], NT, preferred_element_type=F32)
    each(ni, lambda off: gi_rs(off).start())
    inat[...] = it[...].T

    for slot in range(3, len(HOPS)):
        gather_users.arrived(slot)
        user_on(slot, core).start()
    mine = rows(wu, mi)
    each(ni, lambda off: gi_rs(off).wait_recv())
    total = gi_part[mine, :]
    for off in range(1, ni):
        total += gi_recv[off]
    gi[mine, :] = total
    each(ni, lambda off: gi_ag(off, mi).start())

    for slot in range(len(HOPS) + 1):
        user_on(slot, 1 - core).wait_recv()
    for k in range(nk):
        counts_copy(k).wait()

    half_scale = alpha_ref[0] * 0.5

    def coefficients(half_left, part):
        step = 256

        def tile(t):
            cols = slice(t * step, (t + 1) * step)
            s = jnp.dot(half_left, it[:, cols], preferred_element_type=F32)
            a = counts[part, cols].astype(F32) * half_scale
            cf[part, cols] = ((a - 0.5) - (a + 0.5) * jnp.tanh(s)).astype(BF16)

        return [functools.partial(tile, t) for t in range(items // step)]

    def user_pair(k):
        part = rows(pair_u, k)

        def gradient():
            grad = jnp.dot(cf[part, :], inat[...], preferred_element_type=F32)
            lower, upper = grad[:own_u], grad[own_u:]
            keep[k] = jnp.where(core == 0, lower, upper)
            sib_send[k] = jnp.where(core == 0, upper, lower)

        return coefficients(ut[:, part].T * jnp.asarray(0.5, BF16), part) + [gradient]

    def on_to_owner(off):
        k = after(off)
        halves(k).wait_recv()
        pack(keep[k] + sib_recv[k], rs1_send.at[k], own_u)
        rs1(off).start()

    sweep = Sweep(inv_a, inv_u, inv_y)
    def plain_pass(off):
        for work in user_pair(after(off)):
            work()
        halves(after(off)).start()

    def plain_step(off, carry):
        plain_pass(off)
        on_to_owner(off - 1)
        return carry

    plain_pass(1)
    lax.fori_loop(2, AHEAD + 1, plain_step, 0)
    each(ni, lambda off: gi_ag(off, from_item(off)).wait_recv())

    def hessian(gram):
        return 0.25 * gram[...] + jnp.where(eye(d), REG, 0.0)

    sweep.begin(hessian(gi))

    def first_pass(off, carry):
        sweep.block(off - 1 - AHEAD, user_pair(after(off)))
        halves(after(off)).start()
        on_to_owner(off - 1)
        return carry

    def sweep_on(k, carry):
        sweep.block(k)
        return carry

    lax.fori_loop(AHEAD + 1, nk + 1, first_pass, 0)
    lax.fori_loop(nk - AHEAD, nk, sweep_on, 0)
    sweep.end(hessian(gi))

    halves(place).wait_recv()
    grad = keep[place] + sib_recv[place]
    for off in range(1, nk):
        rs1(off).wait_recv()
        grad += unpack(rs1_recv.at[off], own_u)
    own = ut[:, rows(own_u, mi)].T.astype(F32)
    grad = grad - REG * own
    new = own + jnp.dot(grad, inv_a[...], precision=EXACT, preferred_element_type=F32)
    uh[rows(own_u, mi), :] = new.astype(BF16)
    gather_half.start()
    half_on(own_slot, core).start()
    u_new[...] = new.T
    u_out[:, rows(own_u, mi)] = u_new[mine, :]

    def turn(k):
        part = rows(pair_u, k)
        uht[:, part] = uh[part, :].T

    def second_pass(k):
        part = rows(pair_u, k)
        half = uh[part, :]
        for work in coefficients(half * jnp.asarray(0.5, BF16), part):
            work()

    half_on(own_slot, 1 - core).wait_recv()
    second_pass(place)
    turn(place)
    for slot in range(3):
        gather_half.arrived(slot)
        half_on(slot, core).start()
    for slot in range(3):
        half_on(slot, 1 - core).wait_recv()

    def near(t, carry):
        k = chip_at(jnp.where(t == 0, -1, jnp.where(t == 1, 1, 0)), jnp.where(t == 2, 1, 0))
        second_pass(k)
        turn(k)
        return carry

    lax.fori_loop(0, 3, near, 0)
    for slot in range(3, len(HOPS)):
        gather_half.arrived(slot)
        half_on(slot, core).start()
    for slot in range(3, len(HOPS)):
        half_on(slot, 1 - core).wait_recv()

    def far(t):
        return chip_at(jnp.where(t < 2, 2, jnp.where(t == 2, 1, -1)), jnp.where(t == 0, 0, 1))

    def far_turn(t, carry):
        turn(far(t))
        return carry

    def far_pass(t, carry):
        second_pass(far(t))
        return carry

    lax.fori_loop(0, 4, far_turn, 0)
    gu_rows[mu] = jnp.dot(uht[mine, :], uh[...], preferred_element_type=F32)
    each(nu, lambda off: gu_rs(off, mu).start())
    each(ni, lambda off: out_user(off, mi).start())
    lax.fori_loop(0, 4, far_pass, 0)
    each(nu, lambda off: gu_rs(off, from_user(off)).wait_recv())
    total = gu_rows[0]
    for k in range(1, nu):
        total += gu_rows[k]
    gu[mine, :] = total
    each(ni, lambda off: gu_ag(off, mi).start())

    def item_pair(q):
        g = jnp.dot(uht[...], cf[:, rows(pair_i, q)], preferred_element_type=F32)
        g = g.T
        pack(g[:own_i], rs2_send.at[2 * q], own_i)
        pack(g[own_i:], rs2_send.at[2 * q + 1], own_i)

    def item_step(q, carry):
        item_pair(q)
        return carry

    lax.fori_loop(0, i_pairs, item_step, 0)
    each(ni, lambda off: gu_ag(off, from_item(off)).wait_recv())
    each(nu, lambda off: rs2(nu - off).start())
    sweep.begin(hessian(gu))

    lax.fori_loop(0, d // PANEL, sweep_on, 0)
    sweep.end(hessian(gu))

    grad = unpack(rs2_send.at[mu], own_i)
    for off in range(nu - 1, 0, -1):
        rs2(off).wait_recv()
        grad += unpack(rs2_recv.at[off], own_i)
    own = inat[rows(own_i, mu), :].astype(F32)
    grad = grad - REG * own
    new = own + jnp.dot(grad, inv_a[...], precision=EXACT, preferred_element_type=F32)
    i_new[:, :own_i] = new.T
    each(nu, lambda off: out_item(off, mu).start())
    i_out[mu] = i_new[rows(wi, mu), :]

    gather_items.drain()
    gather_users.drain()
    gather_half.drain()

    def drain_item(off):
        gi_rs(off).wait_send()
        gi_ag(off, mi).wait_send()
        gu_ag(off, mi).wait_send()
        out_user(off, mi).wait_send()

    def drain_chip(k):
        halves(k).wait_send()

    def drain_user(off):
        rs2(off).wait_send()
        gu_rs(off, mu).wait_send()

    each(ni, drain_item)
    each(nk, lambda off: rs1(off).wait_send())
    each(nk, drain_chip, 0)
    for slot in range(len(HOPS) + 1):
        user_on(slot, core).wait_send()
        half_on(slot, core).wait_send()
    each(nu, drain_user)
    each(ni, lambda off: out_user(off, from_item(off)).wait_recv())
    each(nu, lambda off: out_item(off, from_user(off)).wait_recv())
    each(nu, lambda off: out_item(off, mu).wait_send())


def on_device(nu, ni, counts, user_factors, item_factors, alpha_scale):
    users, items = counts.shape
    d = user_factors.shape[1] * ni
    nk, slots = ni // 2, len(HOPS)
    wu, wi, own_u, own_i = d // ni, d // nu, users // ni, items // nu
    vmem = pl.BlockSpec(memory_space=pltpu.VMEM)
    spare, dma = pltpu.VMEM, pltpu.SemaphoreType.DMA
    u_out, i_out = pl.pallas_call(
        functools.partial(kernel, nu, ni),
        out_shape=(
            jax.ShapeDtypeStruct((wu, users), F32),
            jax.ShapeDtypeStruct((nu, wi, 2 * LANES), F32),
        ),
        in_specs=[
            pl.BlockSpec(memory_space=pltpu.SMEM), vmem, vmem, pl.BlockSpec(memory_space=pl.ANY),
        ],
        out_specs=(vmem, vmem),
        scratch_shapes=[
            spare((users, items), jnp.int32),
            spare((d, users), BF16), spare((d, items), BF16),
            spare((items, d), BF16),
            spare((users, items), BF16),
            spare((nk, own_u, d), F32), spare((nk, own_u, d), F32), spare((nk, own_u, d), F32),
            spare((nk, own_u + TILE, d), jnp.int16), spare((nk, own_u + TILE, d), jnp.int16),
            spare((d, d), F32), spare((ni, wu, d), F32), spare((d, d), F32),
            spare((users, d), BF16), spare((d, users), BF16), spare((d, own_u), F32),
            spare((nu, wu, d), F32), spare((d, d), F32),
            spare((nu, own_i + TILE, d), jnp.int16), spare((nu, own_i + TILE, d), jnp.int16),
            spare((d, 2 * LANES), F32),
            spare((d, d), F32), spare((d, LANES), F32), spare((PANEL, d), F32),
            dma((nk,)), dma((4, ni)), dma((4, ni)), dma((1, nk)), dma((1, nk)),
            dma((3, slots + 1)), dma((3, slots + 1)), dma((3, nu)), dma((3, nu)),
            dma((3, slots)), dma((3, slots)),
        ],
        compiler_params=pltpu.CompilerParams(
            collective_id=0, has_side_effects=True, vmem_limit_bytes=60 << 20
        ),
    )(alpha_scale, user_factors.T, item_factors.T, counts)

    def lay(u_ref, i_ref, u_to, i_to):
        u_to[...] = u_ref[...]
        for k in range(0, nu, 2):
            pair = jnp.concatenate([i_ref[k][:, :own_i], i_ref[k + 1][:, :own_i]], axis=1)
            i_to[:, k * own_i : (k + 2) * own_i] = pair

    u_new, i_new = pl.pallas_call(
        lay,
        out_shape=(jax.ShapeDtypeStruct((wu, users), F32), jax.ShapeDtypeStruct((wi, items), F32)),
        in_specs=[vmem, vmem],
        out_specs=(vmem, vmem),
    )(u_out, i_out)
    return u_new.T, i_new.T


def solution(mesh):
    in_specs = (P("user", "item"), P("user", "item"), P("item", "user"), P())
    out_specs = (P("user", "item"), P("item", "user"))
    return jax.shard_map(
        functools.partial(on_device, mesh.shape["user"], mesh.shape["item"]),
        mesh=mesh, in_specs=in_specs, out_specs=out_specs, check_vma=False,
    )
```
